512 devices in a mesh: section: 32 (over z, core), dp: 16 (over x, y).
Axes of the slice: x: 4, y: 4, z: 16, core: 2. Of those that a mesh axis runs over, the one named last changes fastest.
Arguments:
- hidden: bfloat16 [256, 8192], P('section', 'dp'), may hold values from -64 to 64, as said below
- head_weight: bfloat16 [65536, 8192], P('section', 'dp'), may hold values from -1 to 1
- labels: int32 [256], replicated, may hold values from 0 to 65535
- loss_grad: float32 [256], replicated, may hold values from 3 to 30
Outputs:
- token_loss: float32 [256], P('dp')
- grad_hidden: bfloat16 [256, 8192], P('section', 'dp')
- grad_weight: bfloat16 [65536, 8192], P('section', 'dp')
The draws below stay inside these ranges and needn't reach their ends.
Inputs may be any that keep to these rules, and one draw needn't show every extreme that they name: `hidden`: hidden states of order one in most rows; some rows may be larger.
All inputs are finite; a program needn't handle non-finite values.
Results may differ from the reference program's by a relative error of at most 0.0048.
Values may be sent and summed in bfloat16 or wider, within the bound.
No kernel may reach another device: no remote copies, remote signals or barrier semaphores. Data moves between devices by JAX's collectives and lax.ppermute only.
A program may use at most 64 MiB of HBM per device.

```python
import math
import jax
import jax.numpy as jnp
import numpy as np
from jax import lax

D = 8192
VOCAB = 65536
TOKENS = 256


def shared_head(key):
    base = jax.random.normal(key, (VOCAB, D), jnp.float32)
    jitter = jax.random.uniform(jax.random.fold_in(key, 5), (VOCAB, 1), jnp.float32, 0.8, 1.25)
    rising = 0.7 * 3.0 ** (jnp.arange(VOCAB, dtype=jnp.float32) / VOCAB)
    sigma = 0.033 * rising[:, None] * jitter
    return base * sigma


def draw_head_weight(key, part):
    weight = shared_head(key)
    return jnp.clip(weight, -1.0, 1.0).astype(jnp.bfloat16)


def draw_hidden(key, part):
    key = jax.random.fold_in(key, 7)
    noise = jax.random.normal(jax.random.fold_in(key, 1), (TOKENS, D), jnp.float32)
    noise = jnp.clip(noise, -6.0, 6.0)
    out = noise
    return out.astype(jnp.bfloat16)


def with_ends(values, stream_key, low, high):
    place = [jax.random.randint(jax.random.fold_in(stream_key, axis), (), 0, length) for axis, length in enumerate(values.shape)]
    longest = values.shape.index(max(values.shape))
    next_to = place[:longest] + [(place[longest] + 1) % values.shape[longest]] + place[longest + 1:]
    return values.at[tuple(place)].set(low).at[tuple(next_to)].set(high)


def rank_bounds(number_of, slope):
    loads = [(1 << 20) // math.isqrt(grade ** slope) + 1 for grade in range(1, number_of + 1)]
    deviation = 1 + sum(loads) // (1 << 30)
    return np.cumsum(np.array([max(1, weight // deviation) for weight in loads]))


def ranked(key, shape, number_of, skew):
    listing = rank_bounds(number_of, skew)
    ticket = jax.random.randint(jax.random.fold_in(key, 1), shape, 0, int(listing[number_of - 1]))
    grade = jnp.searchsorted(jnp.asarray(listing, jnp.int32), ticket, side="right")
    return jax.random.permutation(jax.random.fold_in(key, 2), number_of)[grade].astype(jnp.int32)


def setup_inputs(seed: int = 0) -> dict:
    key_of = jax.random.split(jax.random.key(seed), 5)
    hidden = draw_hidden(jax.random.fold_in(key_of[4], 71), 0)
    head_weight = draw_head_weight(jax.random.fold_in(key_of[4], 71), 0)
    labels = with_ends(ranked(key_of[2], (TOKENS,), VOCAB, 1), jax.random.fold_in(key_of[2], 3), 0, VOCAB - 1).astype(jnp.int32)
    loss_grad = jnp.clip(jnp.exp(jax.random.uniform(key_of[3], (TOKENS,), jnp.float32, math.log(3.0), math.log(30.0))), 3.0, 30.0)
    return dict(hidden=hidden, head_weight=head_weight, labels=labels, loss_grad=loss_grad)


def reference(hidden, head_weight, labels, loss_grad):
    logits = lax.dot_general(hidden, head_weight, (((1,), (1,)), ((), ())), preferred_element_type=jnp.float32)
    top = jnp.max(logits, axis=1)
    total = jnp.sum(jnp.exp(logits - top[:, None]), axis=1)
    columns = jnp.arange(VOCAB, dtype=jnp.int32)
    onehot = (labels[:, None] == columns[None, :]).astype(jnp.float32)
    target = jnp.sum(logits * onehot, axis=1)
    log_total = top + jnp.log(total)
    token_loss = log_total - target
    dlogits = (loss_grad[:, None] * (jnp.exp(logits - log_total[:, None]) - onehot)).astype(jnp.bfloat16)
    grad_hidden = jnp.dot(dlogits, head_weight, preferred_element_type=jnp.float32)
    grad_weight = lax.dot_general(dlogits, hidden, (((0,), (0,)), ((), ())), preferred_element_type=jnp.float32)
    return token_loss, grad_hidden.astype(jnp.bfloat16), grad_weight.astype(jnp.bfloat16)
```

```python
import jax
import jax.numpy as jnp
from jax import lax
from jax.sharding import PartitionSpec as P

F32 = jnp.float32
BF16 = jnp.bfloat16
LANES = 128


def to_bf16(x):
    return lax.reduce_precision(x, 8, 7)


def split3(x):
    a = to_bf16(x)
    b = to_bf16(x - a)
    c = x - a - b
    return a.astype(BF16), b.astype(BF16), c.astype(BF16)


def join3(a, b, c):
    return (a.astype(F32) + b.astype(F32)) + c.astype(F32)


def code(part, row, owner):
    high = to_bf16(part)
    low = jnp.where(owner, row, part - high)
    return high.astype(BF16), low.astype(BF16)


def decode(high, low, owner):
    high, low = high.astype(F32), low.astype(F32)
    return high + jnp.where(owner, 0.0, low), jnp.where(owner, low, 0.0)


def local(hidden, head_weight, labels, loss_grad):
    voc_dev, feat = head_weight.shape
    mine_n = hidden.shape[0]
    n_dp = lax.axis_size("dp")
    n_sec = lax.axis_size("section")
    n_z = n_sec // 2
    half = n_z * mine_n
    tokens = 2 * half
    share = tokens // n_dp
    section = lax.axis_index("section")
    z, core = section // 2, section % 2
    j = lax.axis_index("dp")
    along_z = [[2 * k + c for k in range(n_z)] for c in range(2)]
    swap = [(i, i ^ 1) for i in range(n_sec)]

    def exchange_z(x):
        return lax.all_to_all(x, "section", 0, 0, tiled=True, axis_index_groups=along_z)

    def exchange_dp(x):
        return lax.all_to_all(x, "dp", 0, 0, tiled=True)

    def own_core_first(x):
        x = x.reshape(n_z, 2, mine_n)
        first = jnp.where(core == 0, x[:, 0], x[:, 1])
        second = jnp.where(core == 0, x[:, 1], x[:, 0])
        return jnp.concatenate([first.reshape(half), second.reshape(half)])

    label = own_core_first(labels)
    grad = own_core_first(loss_grad)
    columns = section * voc_dev + jnp.arange(voc_dev, dtype=jnp.int32)

    mine = exchange_z(jnp.broadcast_to(hidden[None], (n_z, mine_n, feat))).reshape(half, feat)
    whole = jnp.concatenate([mine, lax.ppermute(mine, "section", swap)])

    partial = lax.dot_general(
        whole, head_weight, (((1,), (1,)), ((), ())), preferred_element_type=F32
    )
    logits = jnp.sum(exchange_dp(partial.reshape(n_dp, share, voc_dev)), axis=0)
    share_label = lax.dynamic_slice_in_dim(label, j * share, share, 0)
    hot = share_label[:, None] == columns[None, :]
    top = jnp.max(logits, axis=1)
    expo = jnp.exp(logits - top[:, None])
    total = jnp.sum(expo, axis=1)
    target = jnp.sum(jnp.where(hot, logits, 0.0), axis=1)
    soft = jnp.where(hot, 0.0, expo * (1.0 / total)[:, None]).astype(BF16)
    stats = jnp.stack(split3(top + jnp.log(total)) + split3(target), axis=1)
    stats = jnp.pad(stats, ((0, 0), (0, LANES - 6)))
    message = jnp.concatenate([soft, stats], axis=1)
    got = exchange_dp(jnp.broadcast_to(message[None], (n_dp, share, voc_dev + LANES)))
    got = got.reshape(tokens, voc_dev + LANES)
    soft = got[:, :voc_dev]
    log_sum = join3(got[:, voc_dev], got[:, voc_dev + 1], got[:, voc_dev + 2])
    target = join3(got[:, voc_dev + 3], got[:, voc_dev + 4], got[:, voc_dev + 5])

    hot = label[:, None] == columns[None, :]
    part = jnp.dot(soft, head_weight, preferred_element_type=F32)
    row = jnp.dot(hot.astype(BF16), head_weight, preferred_element_type=F32)
    owner = label // voc_dev == section
    high, low = code(part[half:], row[half:], owner[half:, None])
    high, low = lax.ppermute(jnp.concatenate([high, low], axis=1), "section", swap).reshape(
        half, 2, feat
    ).transpose(1, 0, 2)
    other = lax.ppermute(jnp.stack([log_sum, target]), "section", swap)
    other_log, other_target = jnp.roll(other, half, axis=1)
    other_part, other_row = decode(high, low, (label // voc_dev == section + 1 - 2 * core)[:half, None])
    low_log = jnp.where(core == 0, log_sum, other_log)
    high_log = jnp.where(core == 0, other_log, log_sum)
    top = jnp.maximum(low_log, high_log)
    pair_log = top + jnp.log(jnp.exp(low_log - top) + jnp.exp(high_log - top))
    pair_target = target + other_target
    part = (
        part[:half] * jnp.exp(log_sum - pair_log)[:half, None]
        + other_part * jnp.exp(other_log - pair_log)[:half, None]
    )
    row = row[:half] + other_row
    high, low = code(part, row, (label // (2 * voc_dev) == z)[:half, None])
    rows = 2 * mine_n
    stats = jnp.stack(split3(pair_log) + split3(pair_target)).reshape(-1, LANES)
    stats = jnp.pad(stats, ((0, rows - stats.shape[0]), (0, 0)))
    message = jnp.concatenate(
        [high.reshape(n_z, mine_n, feat), low.reshape(n_z, mine_n, feat)], axis=1
    )
    message = jnp.concatenate(
        [message, jnp.broadcast_to(stats[None], (n_z, rows, LANES))], axis=2
    )
    got = exchange_z(message)
    stats = got[:, :, feat:].reshape(n_z, -1)[:, : 6 * tokens].reshape(n_z, 6, tokens)
    logs = join3(stats[:, 0], stats[:, 1], stats[:, 2])
    target = jnp.sum(join3(stats[:, 3], stats[:, 4], stats[:, 5]), axis=0)
    top = jnp.max(logs, axis=0)
    log_total = top + jnp.log(jnp.sum(jnp.exp(logs - top), axis=0))
    loss = log_total - target
    loss = lax.dynamic_slice_in_dim(loss.reshape(2, half), j * (share // 2), share // 2, 1)
    loss = jnp.where(core == 0, loss, loss[::-1]).reshape(share)
    label_grad = grad * (jnp.exp(target - log_total) - 1.0)

    def my_tokens(x):
        return lax.dynamic_slice_in_dim(x, z * mine_n, mine_n, x.ndim - 1)

    owners = my_tokens(label)[None, :] // (2 * voc_dev) == jnp.arange(n_z)[:, None]
    parts, rows_ = decode(got[:, :mine_n, :feat], got[:, mine_n:, :feat], owners[:, :, None])
    weights = jnp.exp(my_tokens(logs) - my_tokens(log_total)[None])
    grad_hidden = (
        my_tokens(grad)[:, None] * jnp.sum(parts * weights[:, :, None], axis=0)
        + my_tokens(label_grad)[:, None] * jnp.sum(rows_, axis=0)
    ).astype(BF16)

    scale = grad * jnp.exp(log_sum - log_total)
    dlogits = jnp.where(hot, label_grad[:, None], soft.astype(F32) * scale[:, None]).astype(BF16)
    grad_weight = lax.dot_general(
        dlogits, whole, (((0,), (0,)), ((), ())), preferred_element_type=F32
    ).astype(BF16)
    return (loss, grad_hidden, grad_weight)


def solution(mesh):
    return jax.shard_map(
        local,
        mesh=mesh,
        in_specs=(P("section", "dp"), P("section", "dp"), P(), P()),
        out_specs=(P("dp"), P("section", "dp"), P("section", "dp")),
        check_vma=False,
    )
```

```python
import functools

import jax
import jax.numpy as jnp
from jax import lax
from jax.experimental import pallas as pl
from jax.experimental.pallas import tpu as pltpu
from jax.sharding import PartitionSpec as P

F32 = jnp.float32
BF16 = jnp.bfloat16
I16 = jnp.int16
I32 = jnp.int32
LANES = 128
CHUNK = 256
STEPS = 32760.0
GRAIN = 64.0
MIB = 1 << 20

SCALARS = pl.BlockSpec(memory_space=pltpu.SMEM)
WHOLE = pl.BlockSpec(memory_space=pltpu.VMEM)


def call(kernel, scalars, args, outs, scratch=(), limit=24, flops=0):
    return pl.pallas_call(
        kernel,
        out_shape=[jax.ShapeDtypeStruct(s, d) for s, d in outs],
        in_specs=[SCALARS] + [WHOLE] * len(args),
        out_specs=[WHOLE] * len(outs),
        scratch_shapes=[pltpu.VMEM(s, d) for s, d in scratch],
        compiler_params=pltpu.CompilerParams(vmem_limit_bytes=limit * MIB),
        cost_estimate=pl.CostEstimate(flops=flops, bytes_accessed=4 * MIB, transcendentals=0),
    )(scalars, *args)


def high_part(x):
    return x.astype(BF16).astype(F32)


def split3(x):
    a = high_part(x)
    b = high_part(x - a)
    return a, b, x - a - b


def lane_block(rows, values):
    lane = lax.broadcasted_iota(I32, (rows, LANES), 1)
    block = jnp.zeros((rows, LANES), F32)
    for k, value in enumerate(values):
        block = jnp.where(lane == k, value, block)
    return block


def join3(block, k):
    return block[:, k : k + 1] + block[:, k + 1 : k + 2] + block[:, k + 2 : k + 3]


def logits_kernel(_, mine, other, weight, out, part):
    half = mine.shape[0]
    voc = weight.shape[0]
    tops = []
    for h, tokens in enumerate((mine, other)):
        top = jnp.zeros((half, LANES), F32)
        for k in range(0, voc, CHUNK):
            block = lax.dot_general(
                tokens[...],
                weight[k : k + CHUNK, :],
                (((1,), (1,)), ((), ())),
                preferred_element_type=F32,
            )
            part[h * half : (h + 1) * half, k : k + CHUNK] = block
            size = jnp.abs(block)
            for c in range(0, CHUNK, LANES):
                top = jnp.maximum(top, size[:, c : c + LANES])
        tops.append(jnp.max(top, axis=1, keepdims=True))
    for h, top in enumerate(tops):
        grade = jnp.ceil(jnp.log2(jnp.maximum(top, 1e-30)) * GRAIN)
        per = STEPS * jnp.exp2(grade * (-1.0 / GRAIN))
        rows = slice(h * half, (h + 1) * half)
        for k in range(0, voc, CHUNK):
            out[rows, k : k + CHUNK] = (
                jnp.round(part[rows, k : k + CHUNK] * per).astype(I32).astype(I16)
            )
        out[rows, voc:] = jnp.broadcast_to(grade, (half, LANES)).astype(I32).astype(I16)


def softmax_kernel(scalars, got, label, out, logits):
    n, share, width = got.shape
    voc = width - LANES
    scales = [
        jnp.exp2(got[i, :, voc:].astype(I32).astype(F32)[:, :1] * (1.0 / GRAIN)) * (1.0 / STEPS)
        for i in range(n)
    ]
    top = jnp.full((share, LANES), -jnp.inf, F32)
    for k in range(0, voc, CHUNK):
        block = jnp.zeros((share, CHUNK), F32)
        for i in range(n):
            block += got[i, :, k : k + CHUNK].astype(I32).astype(F32) * scales[i]
        logits[:, k : k + CHUNK] = block
        for c in range(0, CHUNK, LANES):
            top = jnp.maximum(top, block[:, c : c + LANES])
    top = jnp.max(top, axis=1, keepdims=True)
    total = jnp.zeros((share, CHUNK), F32)
    target = jnp.zeros((share, CHUNK), F32)
    place = label[...] - scalars[0] * voc
    lane = lax.broadcasted_iota(I32, (share, CHUNK), 1)
    for k in range(0, voc, CHUNK):
        block = logits[:, k : k + CHUNK]
        expo = jnp.exp(block - top)
        total += expo
        hot = lane + k == place
        target += jnp.where(hot, block, 0.0)
        logits[:, k : k + CHUNK] = jnp.where(hot, 0.0, expo)
    total = jnp.sum(total, axis=1, keepdims=True)
    target = jnp.sum(target, axis=1, keepdims=True)
    inverse = 1.0 / total
    for k in range(0, voc, CHUNK):
        soft = (logits[:, k : k + CHUNK] * inverse).astype(BF16)
        for i in range(n):
            out[i, :, k : k + CHUNK] = soft
    stats = lane_block(share, split3(top + jnp.log(total)) + split3(target)).astype(BF16)
    for i in range(n):
        out[i, :, voc:] = stats


def partial_kernel(scalars, got, weight, row, label, send, part, stat):
    voc, feat = weight.shape
    half = got.shape[0] // 2
    product = jnp.dot(got[:, :voc], weight[...], preferred_element_type=F32)
    part[...] = product[:half]
    rest = product[half:]
    place = label[half:, :] - scalars[0] * voc
    owner = (place >= 0) & (place < voc)
    high = high_part(rest)
    send[:, :feat] = high.astype(BF16)
    send[:, feat : 2 * feat] = jnp.where(owner, row[half:, :], rest - high).astype(BF16)
    stats = got[:, voc:].astype(F32)
    lane = lax.broadcasted_iota(I32, (half, LANES), 1)
    moved = pltpu.roll(stats[half:], 6, 1)
    send[:, 2 * feat :] = jnp.where(lane < 6, stats[:half], moved).astype(BF16)
    stat[...] = lane_block(2 * half, [join3(stats, 0), join3(stats, 3)])


def pair_kernel(scalars, part, row, stat, got, label, out, rows):
    half, feat = part.shape
    section, core = scalars[0], scalars[2]
    voc = scalars[4]
    n_z = out.shape[0]
    mine_n = half // n_z
    theirs = got[:, 2 * feat :].astype(F32)
    own_log, own_target = stat[:, 0:1], stat[:, 1:2]
    other_log = jnp.concatenate([join3(theirs, 6), join3(theirs, 0)], axis=0)
    other_target = jnp.concatenate([join3(theirs, 9), join3(theirs, 3)], axis=0)
    first = jnp.where(core == 0, own_log, other_log)
    second = jnp.where(core == 0, other_log, own_log)
    top = jnp.maximum(first, second)
    pair_log = top + jnp.log(jnp.exp(first - top) + jnp.exp(second - top))
    pair_target = own_target + other_target
    stats = lane_block(
        2 * half, split3(pair_log) + split3(pair_target) + (own_log, own_target)
    ).T[:8]
    rows[...] = stats
    block = jnp.concatenate([stats[:, :half], stats[:, half:]], axis=0).astype(BF16)
    place = label[:half, :] - (section - core) * voc
    owner = (place >= 0) & (place < 2 * voc)
    own_owner = owner & (place >= core * voc) & (place < (core + 1) * voc)
    other_owner = owner & jnp.logical_not(own_owner)
    low = got[:, feat : 2 * feat].astype(F32)
    other_part = got[:, :feat].astype(F32) + jnp.where(other_owner, 0.0, low)
    total = part[...] * jnp.exp(own_log - pair_log)[:half] + other_part * jnp.exp(
        other_log - pair_log
    )[:half]
    high = high_part(total)
    low = jnp.where(own_owner, row[:half, :], jnp.where(other_owner, low, total - high))
    for i in range(n_z):
        at = slice(i * mine_n, (i + 1) * mine_n)
        out[i, :, :feat] = jnp.concatenate([high[at], low[at]], axis=0).astype(BF16)
        out[i, :, feat:] = block


def tail_kernel(
    scalars, got, soft, rows, mine, other, label, grad, own_label, own_grad, loss, hidden, weight
):
    n_z, twice, width = got.shape
    feat = width - LANES
    mine_n = twice // 2
    half, tokens = mine.shape[0], 2 * mine.shape[0]
    section, z, core, j, voc = (scalars[k] for k in range(5))

    def stat_rows(k):
        both = []
        for h in range(2):
            pieces = [got[:, h * mine_n + k + i, feat:].astype(F32) for i in range(3)]
            both.append(pieces[0] + pieces[1] + pieces[2])
        return jnp.concatenate(both, axis=1)

    logs = stat_rows(0)
    target = jnp.sum(stat_rows(3), axis=0, keepdims=True)
    top = jnp.max(logs, axis=0, keepdims=True)
    log_total = top + jnp.log(jnp.sum(jnp.exp(logs - top), axis=0, keepdims=True))
    label_part = jnp.exp(target - log_total) - 1.0
    losses = log_total - target
    pick = (half - j * (loss.shape[1] // 2)) % half
    first = pltpu.roll(jnp.broadcast_to(losses[:, :half], (8, half)), pick, 1)
    second = pltpu.roll(jnp.broadcast_to(losses[:, half:], (8, half)), pick, 1)
    loss_low = jnp.where(core == 0, first, second)
    loss_high = pltpu.roll(jnp.where(core == 0, second, first), loss.shape[1] // 2, 1)
    lane = lax.broadcasted_iota(I32, (8, half), 1)
    loss[...] = jnp.where(lane < loss.shape[1] // 2, loss_low, loss_high)[:1, : loss.shape[1]]

    shares = jnp.exp(logs - log_total)[:, :half]
    block = jnp.concatenate(
        [shares, jnp.broadcast_to(label_part[:, :half], (half - n_z, half))], axis=0
    )
    block = pltpu.roll(block, (half - z * mine_n) % half, 1).T[:mine_n]
    total = jnp.zeros((mine_n, feat), F32)
    row = jnp.zeros((mine_n, feat), F32)
    for i in range(n_z):
        both = got[i, :, :feat].astype(F32)
        place = own_label[...] - i * 2 * voc
        owner = (place >= 0) & (place < 2 * voc)
        low = both[mine_n:]
        total += (both[:mine_n] + jnp.where(owner, 0.0, low)) * block[:, i : i + 1]
        row += jnp.where(owner, low, 0.0)
    hidden[...] = (own_grad[...] * (total + row * block[:, n_z : n_z + 1])).astype(BF16)

    scale = grad[...] * jnp.exp(rows[6:7, :] - log_total)
    label_grad = grad[...] * label_part
    place = label[...] - section * voc
    tall = weight.shape[0]
    line = lax.broadcasted_iota(I32, (CHUNK, tokens), 0)
    for k in range(0, tall, CHUNK):
        value = soft[k : k + CHUNK, :].astype(F32) * scale
        value = jnp.where(line + k == place, label_grad, value).astype(BF16)
        weight[k : k + CHUNK, :] = (
            jnp.dot(value[:, :half], mine[...], preferred_element_type=F32)
            + jnp.dot(value[:, half:], other[...], preferred_element_type=F32)
        ).astype(BF16)


def local(hidden, head_weight, labels, loss_grad):
    voc, feat = head_weight.shape
    mine_n = hidden.shape[0]
    n_dp = lax.axis_size("dp")
    n_sec = lax.axis_size("section")
    n_z = n_sec // 2
    half = n_z * mine_n
    tokens = 2 * half
    share = tokens // n_dp
    section = lax.axis_index("section")
    z, core = section // 2, section % 2
    j = lax.axis_index("dp")
    scalars = jnp.stack([section, z, core, j, jnp.int32(voc)]).astype(I32)
    along_z = [[2 * k + c for k in range(n_z)] for c in range(2)]
    swap = [(i, i ^ 1) for i in range(n_sec)]
    flops = 2 * tokens * voc * feat

    def exchange_z(x):
        return lax.all_to_all(x, "section", 0, 0, tiled=True, axis_index_groups=along_z)

    def exchange_dp(x):
        return lax.all_to_all(x, "dp", 0, 0, tiled=True)

    def own_core_first(x):
        x = x.reshape(n_z, 2, mine_n)
        first = jnp.where(core == 0, x[:, 0], x[:, 1])
        second = jnp.where(core == 0, x[:, 1], x[:, 0])
        return jnp.concatenate([first.reshape(half), second.reshape(half)])

    label = own_core_first(labels)
    grad = own_core_first(loss_grad)
    label_column = label[:, None]
    share_label = lax.dynamic_slice_in_dim(label, j * share, share, 0)[:, None]
    own_label = lax.dynamic_slice_in_dim(label, z * mine_n, mine_n, 0)[:, None]
    own_grad = lax.dynamic_slice_in_dim(grad, z * mine_n, mine_n, 0)[:, None]
    columns = section * voc + jnp.arange(voc, dtype=I32)

    mine = exchange_z(jnp.broadcast_to(hidden[None], (n_z, mine_n, feat))).reshape(half, feat)
    other = lax.ppermute(mine, "section", swap)

    width = voc + LANES
    (coded,) = call(
        logits_kernel,
        scalars,
        [mine, other, head_weight],
        [((tokens, width), I16)],
        scratch=[((tokens, voc), F32)],
        flops=flops,
    )
    coded = exchange_dp(coded.reshape(n_dp, share, width))
    (message,) = call(
        softmax_kernel,
        scalars,
        [coded, share_label],
        [((n_dp, share, width), BF16)],
        scratch=[((share, voc), F32)],
    )
    got = exchange_dp(message).reshape(tokens, width)

    hot = label[:, None] == columns[None, :]
    row = jnp.dot(hot.astype(BF16), head_weight, preferred_element_type=F32)
    send, part, stat = call(
        partial_kernel,
        scalars,
        [got, head_weight, row, label_column],
        [((half, 2 * feat + LANES), BF16), ((half, feat), F32), ((tokens, LANES), F32)],
        flops=flops,
    )
    theirs = lax.ppermute(send, "section", swap)
    message, rows = call(
        pair_kernel,
        scalars,
        [part, row, stat, theirs, label_column],
        [((n_z, 2 * mine_n, feat + LANES), BF16), ((8, tokens), F32)],
    )
    last = exchange_z(message)
    soft = got[:, :voc].T
    loss, grad_hidden, grad_weight = call(
        tail_kernel,
        scalars,
        [last, soft, rows, mine, other, label[None], grad[None], own_label, own_grad],
        [((1, share), F32), ((mine_n, feat), BF16), ((voc, feat), BF16)],
        flops=flops,
    )
    return (loss.reshape(share), grad_hidden, grad_weight)


def solution(mesh):
    return jax.shard_map(
        local,
        mesh=mesh,
        in_specs=(P("section", "dp"), P("section", "dp"), P(), P()),
        out_specs=(P("dp"), P("section", "dp"), P("section", "dp")),
        check_vma=False,
    )
```

```python
import functools

import jax
import jax.numpy as jnp
from jax import lax
from jax.experimental import pallas as pl
from jax.experimental.pallas import tpu as pltpu
from jax.sharding import PartitionSpec as P

F32 = jnp.float32
BF16 = jnp.bfloat16
I16 = jnp.int16
I32 = jnp.int32
LANES = 128
CHUNK = 256
STEPS = 32760.0
GRAIN = 64.0
MIB = 1 << 20

SCALARS = pl.BlockSpec(memory_space=pltpu.SMEM)
WHOLE = pl.BlockSpec(memory_space=pltpu.VMEM)


def call(kernel, scalars, args, outs, scratch=(), copies=0, flops=0):
    out_specs = [WHOLE] * len(outs)
    scratch_shapes = [pltpu.VMEM(s, d) for s, d in scratch]
    if copies:
        out_specs[-1] = pl.BlockSpec(memory_space=pl.ANY)
        scratch_shapes.append(pltpu.SemaphoreType.DMA((copies,)))
    return pl.pallas_call(
        kernel,
        out_shape=[jax.ShapeDtypeStruct(s, d) for s, d in outs],
        in_specs=[SCALARS] + [WHOLE] * len(args),
        out_specs=out_specs,
        scratch_shapes=scratch_shapes,
        compiler_params=pltpu.CompilerParams(vmem_limit_bytes=16 * MIB),
        cost_estimate=pl.CostEstimate(flops=flops, bytes_accessed=4 * MIB, transcendentals=0),
    )(scalars, *args)


def high_part(x):
    return x.astype(BF16).astype(F32)


def split3(x):
    a = high_part(x)
    b = high_part(x - a)
    return a, b, x - a - b


def lane_block(rows, values):
    lane = lax.broadcasted_iota(I32, (rows, LANES), 1)
    block = jnp.zeros((rows, LANES), F32)
    for k, value in enumerate(values):
        block = jnp.where(lane == k, value, block)
    return block


def join3(block, k):
    return block[k : k + 1] + block[k + 1 : k + 2] + block[k + 2 : k + 3]


def logits_kernel(_, mine, other, weight, out, whole, part):
    half = mine.shape[0]
    voc = weight.shape[1]
    whole[:half, :] = mine[...]
    whole[half:, :] = other[...]
    top = jnp.zeros((2 * half, LANES), F32)
    for k in range(0, voc, CHUNK):
        block = jnp.dot(whole[...], weight[:, k : k + CHUNK], preferred_element_type=F32)
        part[:, k : k + CHUNK] = block
        size = jnp.abs(block)
        for c in range(0, CHUNK, LANES):
            top = jnp.maximum(top, size[:, c : c + LANES])
    top = jnp.max(top, axis=1, keepdims=True)
    grade = jnp.ceil(jnp.log2(jnp.maximum(top, 1e-30)) * GRAIN)
    per = STEPS * jnp.exp2(grade * (-1.0 / GRAIN))
    for k in range(0, voc, CHUNK):
        out[:, k : k + CHUNK] = jnp.round(part[:, k : k + CHUNK] * per).astype(I32).astype(I16)
    out[:, voc:] = jnp.broadcast_to(grade, (2 * half, LANES)).astype(I32).astype(I16)


def softmax_kernel(scalars, got, label, out, logits):
    n, share, width = got.shape
    voc = width - LANES
    scales = [
        jnp.exp2(got[i, :, voc:].astype(I32).astype(F32)[:, :1] * (1.0 / GRAIN)) * (1.0 / STEPS)
        for i in range(n)
    ]
    top = jnp.full((share, LANES), -jnp.inf, F32)
    for k in range(0, voc, CHUNK):
        block = jnp.zeros((share, CHUNK), F32)
        for i in range(n):
            block += got[i, :, k : k + CHUNK].astype(I32).astype(F32) * scales[i]
        logits[:, k : k + CHUNK] = block
        for c in range(0, CHUNK, LANES):
            top = jnp.maximum(top, block[:, c : c + LANES])
    top = jnp.max(top, axis=1, keepdims=True)
    total = jnp.zeros((share, CHUNK), F32)
    target = jnp.zeros((share, CHUNK), F32)
    place = label[...] - scalars[0] * voc
    lane = lax.broadcasted_iota(I32, (share, CHUNK), 1)
    for k in range(0, voc, CHUNK):
        block = logits[:, k : k + CHUNK]
        expo = jnp.exp(block - top)
        total += expo
        hot = lane + k == place
        target += jnp.where(hot, block, 0.0)
        logits[:, k : k + CHUNK] = jnp.where(hot, 0.0, expo)
    total = jnp.sum(total, axis=1, keepdims=True)
    target = jnp.sum(target, axis=1, keepdims=True)
    inverse = 1.0 / total
    for k in range(0, voc, CHUNK):
        soft = (logits[:, k : k + CHUNK] * inverse).astype(BF16)
        for i in range(n):
            out[i, :, k : k + CHUNK] = soft
    stats = lane_block(share, split3(top + jnp.log(total)) + split3(target)).astype(BF16)
    for i in range(n):
        out[i, :, voc:] = stats


def partial_kernel(scalars, got, weight, row, label, send, part, stat):
    voc, feat = weight.shape
    half = got.shape[0] // 2
    stats = got[:, voc:].astype(F32).T[:8]
    send[half:, :LANES] = jnp.concatenate([stats[:, :half], stats[:, half:]], axis=0).astype(BF16)
    stat[...] = jnp.concatenate([join3(stats, 0), join3(stats, 3), stats[:6]], axis=0)
    rest = jnp.dot(got[half:, :voc], weight[...], preferred_element_type=F32)
    place = label[half:, :] - scalars[0] * voc
    owner = (place >= 0) & (place < voc)
    high = rest.astype(BF16)
    send[:half, :feat] = high
    send[:half, feat:] = jnp.where(
        owner, row[half:, :].astype(F32), rest - high.astype(F32)
    ).astype(BF16)
    part[...] = jnp.dot(got[:half, :voc], weight[...], preferred_element_type=F32)


def pair_kernel(scalars, part, row, stat, got, label, out):
    half, feat = part.shape
    section, core = scalars[0], scalars[2]
    voc = scalars[4]
    n_z = out.shape[0]
    mine_n = half // n_z
    theirs = got[half:, :LANES].astype(F32)
    own_log, own_target = stat[0:1, :], stat[1:2, :]
    other_log = jnp.concatenate([join3(theirs, 8), join3(theirs, 0)], axis=1)
    other_target = jnp.concatenate([join3(theirs, 11), join3(theirs, 3)], axis=1)
    first = jnp.where(core == 0, own_log, other_log)
    second = jnp.where(core == 0, other_log, own_log)
    top = jnp.maximum(first, second)
    pair_log = top + jnp.log(jnp.exp(first - top) + jnp.exp(second - top))
    shares = jnp.concatenate(
        [jnp.exp(own_log - pair_log)[:, :half], jnp.exp(other_log - pair_log)[:, :half]], axis=0
    )
    shares = jnp.concatenate([shares] * (half // 2), axis=0).T
    stats = jnp.concatenate(
        split3(pair_log) + split3(own_target + other_target) + (own_log, own_log), axis=0
    )
    block = jnp.concatenate([stats[:, :half], stats[:, half:]], axis=0).astype(BF16)
    place = label[:half, :] - (section - core) * voc
    owner = (place >= 0) & (place < 2 * voc)
    own_owner = owner & (place >= core * voc) & (place < (core + 1) * voc)
    other_owner = owner & jnp.logical_not(own_owner)
    low = got[:half, feat:].astype(F32)
    other_part = got[:half, :feat].astype(F32) + jnp.where(other_owner, 0.0, low)
    total = part[...] * shares[:, 0:1] + other_part * shares[:, 1:2]
    high = high_part(total)
    low = jnp.where(
        own_owner, row[:half, :].astype(F32), jnp.where(other_owner, low, total - high)
    )
    for i in range(n_z):
        at = slice(i * mine_n, (i + 1) * mine_n)
        out[i, :, :feat] = jnp.concatenate([high[at], low[at]], axis=0).astype(BF16)
        out[i, :, feat:] = block


def tail_kernel(
    scalars, got, soft, stat, whole, label, grad, own_label, own_grad, loss, hidden, weight, staged, sems
):
    n_z, twice, width = got.shape
    feat = width - LANES
    mine_n = twice // 2
    tokens = whole.shape[0]
    half = tokens // 2
    section, z, core, j, voc = (scalars[k] for k in range(5))

    def stat_rows(k):
        both = []
        for h in range(2):
            pieces = [got[:, h * mine_n + k + i, feat:].astype(F32) for i in range(3)]
            both.append(pieces[0] + pieces[1] + pieces[2])
        return jnp.concatenate(both, axis=1)

    logs = stat_rows(0)
    target = jnp.sum(stat_rows(3), axis=0, keepdims=True)
    top = jnp.max(logs, axis=0, keepdims=True)
    log_total = top + jnp.log(jnp.sum(jnp.exp(logs - top), axis=0, keepdims=True))
    label_part = jnp.exp(target - log_total) - 1.0
    losses = log_total - target

    scale = grad[...] * jnp.exp(stat[0:1, :] - log_total)
    label_grad = grad[...] * label_part
    place = label[...] - section * voc
    line = lax.broadcasted_iota(I32, (CHUNK, tokens), 0)
    copies = []
    for n, k in enumerate(range(0, weight.shape[0], CHUNK)):
        value = soft[k : k + CHUNK, :].astype(F32) * scale
        value = jnp.where(line + k == place, label_grad, value).astype(BF16)
        staged[k : k + CHUNK, :] = jnp.dot(
            value, whole[...], preferred_element_type=F32
        ).astype(BF16)
        at = pl.ds(k, CHUNK)
        copies.append(pltpu.make_async_copy(staged.at[at], weight.at[at], sems.at[n]))
        copies[-1].start()

    pick = (half - j * (loss.shape[1] // 2)) % half
    first = pltpu.roll(jnp.broadcast_to(losses[:, :half], (8, half)), pick, 1)
    second = pltpu.roll(jnp.broadcast_to(losses[:, half:], (8, half)), pick, 1)
    loss_low = jnp.where(core == 0, first, second)
    loss_high = pltpu.roll(jnp.where(core == 0, second, first), loss.shape[1] // 2, 1)
    lane = lax.broadcasted_iota(I32, (8, half), 1)
    loss[...] = jnp.where(lane < loss.shape[1] // 2, loss_low, loss_high)[:1, : loss.shape[1]]

    shares = jnp.exp(logs - log_total)[:, :half]
    block = jnp.concatenate(
        [shares, jnp.broadcast_to(label_part[:, :half], (half - n_z, half))], axis=0
    )
    block = pltpu.roll(block, (half - z * mine_n) % half, 1).T[:mine_n]
    total = jnp.zeros((mine_n, feat), F32)
    row = jnp.zeros((mine_n, feat), F32)
    for i in range(n_z):
        both = got[i, :, :feat].astype(F32)
        place = own_label[...] - i * 2 * voc
        owner = (place >= 0) & (place < 2 * voc)
        low = both[mine_n:]
        total += (both[:mine_n] + jnp.where(owner, 0.0, low)) * block[:, i : i + 1]
        row += jnp.where(owner, low, 0.0)
    hidden[...] = (own_grad[...] * (total + row * block[:, n_z : n_z + 1])).astype(BF16)
    for copy in copies:
        copy.wait()


def local(hidden, head_weight, labels, loss_grad):
    voc, feat = head_weight.shape
    mine_n = hidden.shape[0]
    n_dp = lax.axis_size("dp")
    n_sec = lax.axis_size("section")
    n_z = n_sec // 2
    half = n_z * mine_n
    tokens = 2 * half
    share = tokens // n_dp
    section = lax.axis_index("section")
    z, core = section // 2, section % 2
    j = lax.axis_index("dp")
    scalars = jnp.stack([section, z, core, j, jnp.int32(voc)]).astype(I32)
    along_z = [[2 * k + c for k in range(n_z)] for c in range(2)]
    swap = [(i, i ^ 1) for i in range(n_sec)]
    flops = 2 * tokens * voc * feat

    def exchange_z(x):
        return lax.all_to_all(x, "section", 0, 0, tiled=True, axis_index_groups=along_z)

    def exchange_dp(x):
        return lax.all_to_all(x, "dp", 0, 0, tiled=True)

    def own_core_first(x):
        x = x.reshape(n_z, 2, mine_n)
        first = jnp.where(core == 0, x[:, 0], x[:, 1])
        second = jnp.where(core == 0, x[:, 1], x[:, 0])
        return jnp.concatenate([first.reshape(half), second.reshape(half)])

    label = own_core_first(labels)
    grad = own_core_first(loss_grad)
    label_column = label[:, None]
    share_label = lax.dynamic_slice_in_dim(label, j * share, share, 0)[:, None]
    own_label = lax.dynamic_slice_in_dim(label, z * mine_n, mine_n, 0)[:, None]
    own_grad = lax.dynamic_slice_in_dim(grad, z * mine_n, mine_n, 0)[:, None]
    columns = section * voc + jnp.arange(voc, dtype=I32)

    mine = exchange_z(jnp.broadcast_to(hidden[None], (n_z, mine_n, feat))).reshape(half, feat)
    hot = label[:, None] == columns[None, :]
    row = jnp.dot(hot.astype(BF16), head_weight, preferred_element_type=F32).astype(BF16)
    ready = (mine, row, head_weight.T, label, grad, label_column, share_label, own_label, own_grad)
    ready = lax.optimization_barrier(ready)
    mine, row, tall, label, grad, label_column, share_label, own_label, own_grad = ready
    other = lax.ppermute(mine, "section", swap)

    width = voc + LANES
    coded, whole = call(
        logits_kernel,
        scalars,
        [mine, other, tall],
        [((tokens, width), I16), ((tokens, feat), BF16)],
        scratch=[((tokens, voc), F32)],
        flops=flops,
    )
    coded = exchange_dp(coded.reshape(n_dp, share, width))
    (message,) = call(
        softmax_kernel,
        scalars,
        [coded, share_label],
        [((n_dp, share, width), BF16)],
        scratch=[((share, voc), F32)],
    )
    got = exchange_dp(message).reshape(tokens, width)

    send, part, stat = call(
        partial_kernel,
        scalars,
        [got, head_weight, row, label_column],
        [((half + 16, 2 * feat), BF16), ((half, feat), F32), ((8, tokens), F32)],
        flops=flops,
    )
    theirs = lax.ppermute(send, "section", swap)
    (message,) = call(
        pair_kernel,
        scalars,
        [part, row, stat, theirs, label_column],
        [((n_z, 2 * mine_n, feat + LANES), BF16)],
    )
    last = exchange_z(message)
    soft = got[:, :voc].T
    loss, grad_hidden, grad_weight = call(
        tail_kernel,
        scalars,
        [last, soft, stat, whole, label[None], grad[None], own_label, own_grad],
        [((1, share), F32), ((mine_n, feat), BF16), ((voc, feat), BF16)],
        scratch=[((voc, feat), BF16)],
        copies=voc // CHUNK,
        flops=flops,
    )
    return (loss.reshape(share), grad_hidden, grad_weight)


def solution(mesh):
    return jax.shard_map(
        local,
        mesh=mesh,
        in_specs=(P("section", "dp"), P("section", "dp"), P(), P()),
        out_specs=(P("dp"), P("section", "dp"), P("section", "dp")),
        check_vma=False,
    )
```

```python
import functools

import jax
import jax.numpy as jnp
from jax import lax
from jax.experimental import pallas as pl
from jax.experimental.pallas import tpu as pltpu
from jax.sharding import PartitionSpec as P

F32 = jnp.float32
BF16 = jnp.bfloat16
I16 = jnp.int16
I32 = jnp.int32
LANES = 128
CHUNK = 256
SPACE = 32
STEPS = 32760.0
GRAIN = 64.0
MIB = 1 << 20

SCALARS = pl.BlockSpec(memory_space=pltpu.SMEM)
WHOLE = pl.BlockSpec(memory_space=pltpu.VMEM)


def call(kernel, scalars, args, outs, scratch=(), copies=0, flops=0):
    out_specs = [WHOLE] * len(outs)
    scratch_shapes = [pltpu.VMEM(s, d) for s, d in scratch]
    if copies:
        out_specs[-1] = pl.BlockSpec(memory_space=pl.ANY)
        scratch_shapes.append(pltpu.SemaphoreType.DMA((copies,)))
    return pl.pallas_call(
        kernel,
        out_shape=[jax.ShapeDtypeStruct(s, d) for s, d in outs],
        in_specs=[SCALARS] * len(scalars) + [WHOLE] * len(args),
        out_specs=out_specs,
        scratch_shapes=scratch_shapes,
        compiler_params=pltpu.CompilerParams(vmem_limit_bytes=16 * MIB),
        cost_estimate=pl.CostEstimate(flops=flops, bytes_accessed=4 * MIB, transcendentals=0),
    )(*scalars, *args)


def high_part(x):
    return x.astype(BF16).astype(F32)


def split3(x):
    a = high_part(x)
    b = high_part(x - a)
    return a, b, x - a - b


def lane_block(rows, values):
    lane = lax.broadcasted_iota(I32, (rows, LANES), 1)
    block = jnp.zeros((rows, LANES), F32)
    for k, value in enumerate(values):
        block = jnp.where(lane == k, value, block)
    return block


def join3(block, k):
    return block[k : k + 1] + block[k + 1 : k + 2] + block[k + 2 : k + 3]


def logits_kernel(mine, other, weight, out, whole, part):
    half = mine.shape[0]
    voc = weight.shape[1]
    whole[:half, :] = mine[...]
    whole[half:, :] = other[...]
    top = jnp.zeros((2 * half, LANES), F32)
    for k in range(0, voc, CHUNK):
        block = jnp.dot(whole[...], weight[:, k : k + CHUNK], preferred_element_type=F32)
        part[:, k : k + CHUNK] = block
        size = jnp.abs(block)
        for c in range(0, CHUNK, LANES):
            top = jnp.maximum(top, size[:, c : c + LANES])
    top = jnp.max(top, axis=1, keepdims=True)
    grade = jnp.ceil(jnp.log2(jnp.maximum(top, 1e-30)) * GRAIN)
    per = STEPS * jnp.exp2(grade * (-1.0 / GRAIN))
    for k in range(0, voc, CHUNK):
        out[:, k : k + CHUNK] = jnp.round(part[:, k : k + CHUNK] * per).astype(I32).astype(I16)
    out[:, voc:] = jnp.broadcast_to(grade, (2 * half, LANES)).astype(I32).astype(I16)


def softmax_kernel(scalars, labels, got, out, logits):
    n, share, width = got.shape
    section, core, j, mine_n = scalars[0], scalars[2], scalars[3], scalars[5]
    voc = width - LANES
    scales = [
        jnp.exp2(got[i, :, voc:].astype(I32).astype(F32)[:, :1] * (1.0 / GRAIN)) * (1.0 / STEPS)
        for i in range(n)
    ]
    top = jnp.full((share, LANES), -jnp.inf, F32)
    for k in range(0, voc, CHUNK):
        block = jnp.zeros((share, CHUNK), F32)
        for i in range(n):
            block += got[i, :, k : k + CHUNK].astype(I32).astype(F32) * scales[i]
        logits[:, k : k + CHUNK] = block
        for c in range(0, CHUNK, LANES):
            top = jnp.maximum(top, block[:, c : c + LANES])
    top = jnp.max(top, axis=1, keepdims=True)
    total = jnp.zeros((share, CHUNK), F32)
    target = jnp.zeros((share, CHUNK), F32)
    sublane = lax.broadcasted_iota(I32, (share, 1), 0)
    place = jnp.zeros((share, 1), I32)
    for r in range(share):
        index = j * share + r
        side = index // (n * share // 2)
        index = index - side * (n * share // 2)
        first = core + side - 2 * core * side
        token = 2 * mine_n * (index // mine_n) + first * mine_n + index % mine_n
        place = jnp.where(sublane == r, labels[token], place)
    place = place - section * voc
    lane = lax.broadcasted_iota(I32, (share, CHUNK), 1)
    for k in range(0, voc, CHUNK):
        block = logits[:, k : k + CHUNK]
        expo = jnp.exp(block - top)
        total += expo
        hot = lane + k == place
        target += jnp.where(hot, block, 0.0)
        logits[:, k : k + CHUNK] = jnp.where(hot, 0.0, expo)
    total = jnp.sum(total, axis=1, keepdims=True)
    target = jnp.sum(target, axis=1, keepdims=True)
    inverse = 1.0 / total
    for k in range(0, voc, CHUNK):
        soft = (logits[:, k : k + CHUNK] * inverse).astype(BF16)
        for i in range(n):
            out[i, :, k : k + CHUNK] = soft
    stats = lane_block(share, split3(top + jnp.log(total)) + split3(target)).astype(BF16)
    for i in range(n):
        out[i, :, voc:] = stats


def partial_kernel(got, weight, send, part, stat):
    voc, feat = weight.shape
    half = got.shape[0] // 2
    stats = got[:, voc:].astype(F32).T[:8]
    send[half:, :LANES] = jnp.concatenate([stats[:, :half], stats[:, half:]], axis=0).astype(BF16)
    stat[...] = jnp.concatenate([join3(stats, 0), join3(stats, 3), stats[:6]], axis=0)
    rest = jnp.dot(got[half:, :voc], weight[...], preferred_element_type=F32)
    high = rest.astype(BF16)
    send[:half, :feat] = high
    send[:half, feat:] = (rest - high.astype(F32)).astype(BF16)
    part[...] = jnp.dot(got[:half, :voc], weight[...], preferred_element_type=F32)


def pair_kernel(scalars, part, stat, got, out):
    half, feat = part.shape
    core, j = scalars[2], scalars[3]
    n_z, mine_n, _ = out.shape
    theirs = got[half:, :LANES].astype(F32)
    own_log, own_target = stat[0:1, :], stat[1:2, :]
    other_log = jnp.concatenate([join3(theirs, 8), join3(theirs, 0)], axis=1)
    other_target = jnp.concatenate([join3(theirs, 11), join3(theirs, 3)], axis=1)
    first = jnp.where(core == 0, own_log, other_log)
    second = jnp.where(core == 0, other_log, own_log)
    top = jnp.maximum(first, second)
    pair_log = top + jnp.log(jnp.exp(first - top) + jnp.exp(second - top))
    shares = jnp.concatenate(
        [jnp.exp(own_log - pair_log)[:, :half], jnp.exp(other_log - pair_log)[:, :half]], axis=0
    )
    shares = jnp.concatenate([shares] * (half // 2), axis=0).T
    total = (
        part[...] * shares[:, 0:1]
        + (got[:half, :feat].astype(F32) + got[:half, feat:].astype(F32)) * shares[:, 1:2]
    )
    logs = split3(pair_log)
    logs = [x[:, h * half : (h + 1) * half] for h in range(2) for x in logs]
    targets = jnp.concatenate(split3(own_target + other_target), axis=0)
    targets = jnp.concatenate([targets] * 3, axis=0)[:8]
    mine, other = targets[:, :half], targets[:, half:]
    lane = lax.broadcasted_iota(I32, (1, half), 1)
    base = jnp.zeros((1, half), F32)
    for k in range(3):
        for n, x in enumerate((mine, other)):
            at = SPACE * k + (n + 1) * mine_n
            moved = pltpu.roll(x, (half + at - mine_n * j) % half, 1)[k : k + 1]
            base = jnp.where((lane >= at) & (lane < at + mine_n), moved, base)
    for i in range(n_z):
        row = base
        for k in range(3):
            at = SPACE * k
            moved = pltpu.roll(mine, (half + at - mine_n * i) % half, 1)[k : k + 1]
            row = jnp.where((lane >= at) & (lane < at + mine_n), moved, row)
        out[i, :, :feat] = total[i * mine_n : (i + 1) * mine_n].astype(BF16)
        out[i, :, feat:] = jnp.concatenate(logs + [row, row], axis=0).astype(BF16)


def tail_kernel(
    scalars,
    loss_grad,
    got,
    soft,
    stat,
    whole,
    label,
    grad,
    label_row,
    loss,
    hidden,
    weight,
    staged,
    sems,
):
    n_z, mine_n, width = got.shape
    feat = width - LANES
    tokens = whole.shape[0]
    half = tokens // 2
    section, z, core = scalars[0], scalars[1], scalars[2]
    j, voc = scalars[3], scalars[4]
    pieces = [got[:, k, feat:].astype(F32) for k in range(7)]
    logs = jnp.concatenate(
        [pieces[0] + pieces[1] + pieces[2], pieces[3] + pieces[4] + pieces[5]], axis=1
    )
    top = jnp.max(logs, axis=0, keepdims=True)
    log_total = top + jnp.log(jnp.sum(jnp.exp(logs - top), axis=0, keepdims=True))

    scale = grad[...] * jnp.exp(stat[0:1, :] - log_total)
    label_grad = grad[...] * (jnp.exp(stat[1:2, :] - log_total) - 1.0)
    place = label[...] - section * voc
    line = lax.broadcasted_iota(I32, (CHUNK, tokens), 0)
    copies = []
    for n, k in enumerate(range(0, weight.shape[0], CHUNK)):
        value = soft[k : k + CHUNK, :].astype(F32) * scale
        value = jnp.where(line + k == place, label_grad, value).astype(BF16)
        staged[k : k + CHUNK, :] = jnp.dot(
            value, whole[...], preferred_element_type=F32
        ).astype(BF16)
        at = pl.ds(k, CHUNK)
        copies.append(pltpu.make_async_copy(staged.at[at], weight.at[at], sems.at[n]))
        copies[-1].start()

    target = (
        pieces[6]
        + pltpu.roll(pieces[6], half - SPACE, 1)
        + pltpu.roll(pieces[6], half - 2 * SPACE, 1)
    )
    target = jnp.broadcast_to(jnp.sum(target, axis=0, keepdims=True), (8, half))
    lane = lax.broadcasted_iota(I32, (8, half), 1)
    mine, other = (
        jnp.broadcast_to(x, (8, half)) for x in (log_total[:, :half], log_total[:, half:])
    )
    first = pltpu.roll(mine, (half - mine_n * j) % half, 1) - pltpu.roll(target, half - mine_n, 1)
    second = pltpu.roll(other, (half - mine_n * j) % half, 1) - pltpu.roll(
        target, half - 2 * mine_n, 1
    )
    low = jnp.where(core == 0, first, second)
    high = pltpu.roll(jnp.where(core == 0, second, first), mine_n, 1)
    loss[...] = jnp.where(lane < mine_n, low, high)[:1, : loss.shape[1]]

    back = (half - mine_n * z) % half
    shares = pltpu.roll(jnp.exp(logs[:, :half] - log_total[:, :half]), back, 1)
    label_part = jnp.exp(target - pltpu.roll(mine, back, 1)) - 1.0
    block = [shares] + [label_part] * ((half - n_z) // 8)
    block = jnp.concatenate(block, axis=0).T[:mine_n]
    sublane = lax.broadcasted_iota(I32, (mine_n, 1), 0)
    own_grad = jnp.zeros((mine_n, 1), F32)
    for r in range(mine_n):
        own_grad = jnp.where(sublane == r, loss_grad[section * mine_n + r], own_grad)
    total = label_row[...].astype(F32) * block[:, n_z : n_z + 1]
    for i in range(n_z):
        total += got[i, :, :feat].astype(F32) * block[:, i : i + 1]
    hidden[...] = (own_grad * total).astype(BF16)
    for copy in copies:
        copy.wait()


def local(hidden, head_weight, labels, loss_grad):
    voc, feat = head_weight.shape
    mine_n = hidden.shape[0]
    n_dp = lax.axis_size("dp")
    n_sec = lax.axis_size("section")
    n_z = n_sec // 2
    half = n_z * mine_n
    tokens = 2 * half
    share = tokens // n_dp
    section = lax.axis_index("section")
    z, core = section // 2, section % 2
    j = lax.axis_index("dp")
    scalars = jnp.stack([section, z, core, j, jnp.int32(voc), jnp.int32(mine_n)]).astype(I32)
    along_z = [[2 * k + c for k in range(n_z)] for c in range(2)]
    swap = [(i, i ^ 1) for i in range(n_sec)]
    flops = 2 * tokens * voc * feat

    def exchange_z(x):
        return lax.all_to_all(x, "section", 0, 0, tiled=True, axis_index_groups=along_z)

    def exchange_dp(x):
        return lax.all_to_all(x, "dp", 0, 0, tiled=True)

    def own_core_first(x):
        x = x.reshape(n_z, 2, mine_n)
        first = jnp.where(core == 0, x[:, 0], x[:, 1])
        second = jnp.where(core == 0, x[:, 1], x[:, 0])
        return jnp.concatenate([first.reshape(half), second.reshape(half)])

    label = own_core_first(labels)
    grad = own_core_first(loss_grad)
    columns = section * voc + jnp.arange(voc, dtype=I32)

    mine = exchange_z(jnp.broadcast_to(hidden[None], (n_z, mine_n, feat))).reshape(half, feat)
    hot = labels[:, None] == columns[None, :]
    rows = jnp.dot(hot.astype(BF16), head_weight, preferred_element_type=F32).astype(BF16)
    ready = (mine, rows, head_weight.T, label, grad)
    mine, rows, tall, label, grad = lax.optimization_barrier(ready)
    label_row = lax.psum_scatter(rows, "section", scatter_dimension=0, tiled=True)
    other = lax.ppermute(mine, "section", swap)

    width = voc + LANES
    coded, whole = call(
        logits_kernel,
        [],
        [mine, other, tall],
        [((tokens, width), I16), ((tokens, feat), BF16)],
        scratch=[((tokens, voc), F32)],
        flops=flops,
    )
    coded = exchange_dp(coded.reshape(n_dp, share, width))
    (message,) = call(
        softmax_kernel,
        [scalars, labels],
        [coded],
        [((n_dp, share, width), BF16)],
        scratch=[((share, voc), F32)],
    )
    got = exchange_dp(message).reshape(tokens, width)

    send, part, stat = call(
        partial_kernel,
        [],
        [got, head_weight],
        [((half + 16, 2 * feat), BF16), ((half, feat), F32), ((8, tokens), F32)],
        flops=flops,
    )
    theirs = lax.ppermute(send, "section", swap)
    (message,) = call(
        pair_kernel,
        [scalars],
        [part, stat, theirs],
        [((n_z, mine_n, feat + LANES), BF16)],
    )
    last = exchange_z(message)
    soft = got[:, :voc].T
    loss, grad_hidden, grad_weight = call(
        tail_kernel,
        [scalars, loss_grad],
        [last, soft, stat, whole, label[None], grad[None], label_row],
        [((1, share), F32), ((mine_n, feat), BF16), ((voc, feat), BF16)],
        scratch=[((voc, feat), BF16)],
        copies=voc // CHUNK,
        flops=flops,
    )
    return (loss.reshape(share), grad_hidden, grad_weight)


def solution(mesh):
    return jax.shard_map(
        local,
        mesh=mesh,
        in_specs=(P("section", "dp"), P("section", "dp"), P(), P()),
        out_specs=(P("dp"), P("section", "dp"), P("section", "dp")),
        check_vma=False,
    )
```

```python
import functools

import jax
import jax.numpy as jnp
from jax import lax
from jax.experimental import pallas as pl
from jax.experimental.pallas import tpu as pltpu
from jax.sharding import PartitionSpec as P

F32 = jnp.float32
BF16 = jnp.bfloat16
I16 = jnp.int16
I32 = jnp.int32
LANES = 128
CHUNK = 256
OWN = 8
SPACE = 32
STEPS = 32760.0
GRAIN = 64.0
MIB = 1 << 20

SCALARS = pl.BlockSpec(memory_space=pltpu.SMEM)
WHOLE = pl.BlockSpec(memory_space=pltpu.VMEM)


def call(kernel, scalars, args, outs, left=(), scratch=(), copies=0, copies_out=False, flops=0):
    anywhere = pl.BlockSpec(memory_space=pl.ANY)
    out_specs = [WHOLE] * len(outs)
    scratch_shapes = [pltpu.VMEM(s, d) for s, d in scratch]
    if copies_out:
        out_specs[-1] = anywhere
    if copies:
        scratch_shapes.append(pltpu.SemaphoreType.DMA((copies,)))
    return pl.pallas_call(
        kernel,
        out_shape=[jax.ShapeDtypeStruct(s, d) for s, d in outs],
        in_specs=[SCALARS] * len(scalars) + [WHOLE] * len(args) + [anywhere] * len(left),
        out_specs=out_specs,
        scratch_shapes=scratch_shapes,
        compiler_params=pltpu.CompilerParams(vmem_limit_bytes=16 * MIB),
        cost_estimate=pl.CostEstimate(flops=flops, bytes_accessed=4 * MIB, transcendentals=0),
    )(*scalars, *args, *left)


def high_part(x):
    return x.astype(BF16).astype(F32)


def split3(x):
    a = high_part(x)
    b = high_part(x - a)
    return a, b, x - a - b


def lane_block(rows, values):
    lane = lax.broadcasted_iota(I32, (rows, LANES), 1)
    block = jnp.zeros((rows, LANES), F32)
    for k, value in enumerate(values):
        block = jnp.where(lane == k, value, block)
    return block


def join3(block, k):
    return block[k : k + 1] + block[k + 1 : k + 2] + block[k + 2 : k + 3]


def logits_kernel(mine, other, weight, out, whole, part):
    half = mine.shape[0]
    voc = weight.shape[1]
    whole[:half, :] = mine[...]
    whole[half:, :] = other[...]
    top = jnp.zeros((2 * half, LANES), F32)
    for k in range(0, voc, CHUNK):
        block = jnp.dot(whole[...], weight[:, k : k + CHUNK], preferred_element_type=F32)
        part[:, k : k + CHUNK] = block
        size = jnp.abs(block)
        for c in range(0, CHUNK, LANES):
            top = jnp.maximum(top, size[:, c : c + LANES])
    top = jnp.max(top, axis=1, keepdims=True)
    grade = jnp.ceil(jnp.log2(jnp.maximum(top, 1e-30)) * GRAIN)
    per = STEPS * jnp.exp2(grade * (-1.0 / GRAIN))
    for k in range(0, voc, CHUNK):
        out[:, k : k + CHUNK] = jnp.round(part[:, k : k + CHUNK] * per).astype(I32).astype(I16)
    out[:, voc:] = jnp.broadcast_to(grade, (2 * half, LANES)).astype(I32).astype(I16)


def softmax_kernel(scalars, labels, got, out, logits):
    n, share, width = got.shape
    section, core, j, mine_n = scalars[0], scalars[2], scalars[3], scalars[5]
    voc = width - LANES
    scales = [
        jnp.exp2(got[i, :, voc:].astype(I32).astype(F32)[:, :1] * (1.0 / GRAIN)) * (1.0 / STEPS)
        for i in range(n)
    ]
    top = jnp.full((share, LANES), -jnp.inf, F32)
    for k in range(0, voc, CHUNK):
        block = jnp.zeros((share, CHUNK), F32)
        for i in range(n):
            block += got[i, :, k : k + CHUNK].astype(I32).astype(F32) * scales[i]
        logits[:, k : k + CHUNK] = block
        for c in range(0, CHUNK, LANES):
            top = jnp.maximum(top, block[:, c : c + LANES])
    top = jnp.max(top, axis=1, keepdims=True)
    total = jnp.zeros((share, CHUNK), F32)
    target = jnp.zeros((share, CHUNK), F32)
    sublane = lax.broadcasted_iota(I32, (share, 1), 0)
    place = jnp.zeros((share, 1), I32)
    for r in range(share):
        index = j * share + r
        side = index // (n * share // 2)
        index = index - side * (n * share // 2)
        first = core + side - 2 * core * side
        token = 2 * mine_n * (index // mine_n) + first * mine_n + index % mine_n
        place = jnp.where(sublane == r, labels[token], place)
    place = place - section * voc
    lane = lax.broadcasted_iota(I32, (share, CHUNK), 1)
    for k in range(0, voc, CHUNK):
        block = logits[:, k : k + CHUNK]
        expo = jnp.exp(block - top)
        total += expo
        hot = lane + k == place
        target += jnp.where(hot, block, 0.0)
        logits[:, k : k + CHUNK] = jnp.where(hot, 0.0, expo)
    total = jnp.sum(total, axis=1, keepdims=True)
    target = jnp.sum(target, axis=1, keepdims=True)
    inverse = 1.0 / total
    for k in range(0, voc, CHUNK):
        soft = (logits[:, k : k + CHUNK] * inverse).astype(BF16)
        for i in range(n):
            out[i, :, k : k + CHUNK] = soft
    stats = lane_block(share, split3(top + jnp.log(total)) + split3(target)).astype(BF16)
    for i in range(n):
        out[i, :, voc:] = stats


def partial_kernel(got, weight, rows, send, part, stat, sems):
    voc, feat = weight.shape
    half = got.shape[0] // 2
    copy = pltpu.make_async_copy(
        rows.at[pl.ds(half, half)], send.at[pl.ds(0, half), pl.ds(feat, feat)], sems.at[0]
    )
    copy.start()
    stats = got[:, voc:].astype(F32).T[:8]
    send[half:, :LANES] = jnp.concatenate([stats[:, :half], stats[:, half:]], axis=0).astype(BF16)
    stat[...] = jnp.concatenate([join3(stats, 0), join3(stats, 3), stats[:6]], axis=0)
    send[:half, :feat] = jnp.dot(
        got[half:, :voc], weight[...], preferred_element_type=F32
    ).astype(BF16)
    part[...] = jnp.dot(got[:half, :voc], weight[...], preferred_element_type=F32)
    copy.wait()


def pair_kernel(scalars, part, stat, got, rows, out, own_rows, sems):
    half, feat = part.shape
    core, j, mine_n = scalars[2], scalars[3], OWN
    n_z = out.shape[0]
    copy = pltpu.make_async_copy(rows.at[pl.ds(0, half)], own_rows, sems.at[0])
    copy.start()
    theirs = got[half:, :LANES].astype(F32)
    own_log, own_target = stat[0:1, :], stat[1:2, :]
    other_log = jnp.concatenate([join3(theirs, 8), join3(theirs, 0)], axis=1)
    other_target = jnp.concatenate([join3(theirs, 11), join3(theirs, 3)], axis=1)
    first = jnp.where(core == 0, own_log, other_log)
    second = jnp.where(core == 0, other_log, own_log)
    top = jnp.maximum(first, second)
    pair_log = top + jnp.log(jnp.exp(first - top) + jnp.exp(second - top))
    shares = jnp.concatenate(
        [jnp.exp(own_log - pair_log)[:, :half], jnp.exp(other_log - pair_log)[:, :half]], axis=0
    )
    shares = jnp.concatenate([shares] * (half // 2), axis=0).T
    total = part[...] * shares[:, 0:1] + got[:half, :feat].astype(F32) * shares[:, 1:2]
    logs = split3(pair_log)
    logs = [x[:, h * half : (h + 1) * half] for h in range(2) for x in logs]
    targets = jnp.concatenate(split3(own_target + other_target), axis=0)
    targets = jnp.concatenate([targets] * 3, axis=0)[:8]
    mine, other = targets[:, :half], targets[:, half:]
    lane = lax.broadcasted_iota(I32, (1, half), 1)
    base = jnp.zeros((1, half), F32)
    for k in range(3):
        for n, x in enumerate((mine, other)):
            at = SPACE * k + (n + 1) * mine_n
            moved = pltpu.roll(x, (half + at - mine_n * j) % half, 1)[k : k + 1]
            base = jnp.where((lane >= at) & (lane < at + mine_n), moved, base)
    copy.wait()
    label_rows = own_rows[...].astype(F32) + got[:half, feat:].astype(F32)
    for i in range(n_z):
        row = base
        for k in range(3):
            at = SPACE * k
            moved = pltpu.roll(mine, (half + at - mine_n * i) % half, 1)[k : k + 1]
            row = jnp.where((lane >= at) & (lane < at + mine_n), moved, row)
        at = slice(i * mine_n, (i + 1) * mine_n)
        for n, k in enumerate(range(0, feat, LANES)):
            here = slice(n * mine_n, (n + 1) * mine_n)
            out[i, here, :] = total[at, k : k + LANES].astype(BF16)
            here = slice(here.start + feat // LANES * mine_n, here.stop + feat // LANES * mine_n)
            out[i, here, :] = label_rows[at, k : k + LANES].astype(BF16)
        out[i, here.stop :, :] = jnp.concatenate(logs + [row, row], axis=0).astype(BF16)


def tail_kernel(
    scalars,
    loss_grad,
    got,
    soft,
    stat,
    whole,
    label,
    grad,
    loss,
    hidden,
    weight,
    staged,
    sems,
):
    n_z, mine_n = got.shape[0], hidden.shape[0]
    tokens, feat = whole.shape
    tiles = feat // LANES
    half = tokens // 2
    section, z, core = scalars[0], scalars[1], scalars[2]
    j, voc = scalars[3], scalars[4]
    pieces = [got[:, 2 * tiles * mine_n + k, :].astype(F32) for k in range(7)]
    logs = jnp.concatenate(
        [pieces[0] + pieces[1] + pieces[2], pieces[3] + pieces[4] + pieces[5]], axis=1
    )
    top = jnp.max(logs, axis=0, keepdims=True)
    log_total = top + jnp.log(jnp.sum(jnp.exp(logs - top), axis=0, keepdims=True))

    scale = grad[...] * jnp.exp(stat[0:1, :] - log_total)
    label_grad = grad[...] * (jnp.exp(stat[1:2, :] - log_total) - 1.0)
    place = label[...] - section * voc
    line = lax.broadcasted_iota(I32, (CHUNK, tokens), 0)
    copies = []
    for n, k in enumerate(range(0, weight.shape[0], CHUNK)):
        value = soft[k : k + CHUNK, :].astype(F32) * scale
        value = jnp.where(line + k == place, label_grad, value).astype(BF16)
        staged[k : k + CHUNK, :] = jnp.dot(
            value, whole[...], preferred_element_type=F32
        ).astype(BF16)
        at = pl.ds(k, CHUNK)
        copies.append(pltpu.make_async_copy(staged.at[at], weight.at[at], sems.at[n]))
        copies[-1].start()

    target = (
        pieces[6]
        + pltpu.roll(pieces[6], half - SPACE, 1)
        + pltpu.roll(pieces[6], half - 2 * SPACE, 1)
    )
    target = jnp.broadcast_to(jnp.sum(target, axis=0, keepdims=True), (8, half))
    lane = lax.broadcasted_iota(I32, (8, half), 1)
    mine, other = (
        jnp.broadcast_to(x, (8, half)) for x in (log_total[:, :half], log_total[:, half:])
    )
    first = pltpu.roll(mine, (half - mine_n * j) % half, 1) - pltpu.roll(target, half - mine_n, 1)
    second = pltpu.roll(other, (half - mine_n * j) % half, 1) - pltpu.roll(
        target, half - 2 * mine_n, 1
    )
    low = jnp.where(core == 0, first, second)
    high = pltpu.roll(jnp.where(core == 0, second, first), mine_n, 1)
    loss[...] = jnp.where(lane < mine_n, low, high)[:1, : loss.shape[1]]

    back = (half - mine_n * z) % half
    shares = pltpu.roll(jnp.exp(logs[:, :half] - log_total[:, :half]), back, 1)
    label_part = jnp.exp(target - pltpu.roll(mine, back, 1)) - 1.0
    block = [shares] + [label_part] * ((half - n_z) // 8)
    block = jnp.concatenate(block, axis=0).T[:mine_n]
    sublane = lax.broadcasted_iota(I32, (mine_n, 1), 0)
    own_grad = jnp.zeros((mine_n, 1), F32)
    for r in range(mine_n):
        own_grad = jnp.where(sublane == r, loss_grad[section * mine_n + r], own_grad)
    for n in range(tiles):
        part = jnp.zeros((mine_n, LANES), F32)
        row = jnp.zeros((mine_n, LANES), F32)
        for i in range(n_z):
            part += got[i, n * mine_n : (n + 1) * mine_n, :].astype(F32) * block[:, i : i + 1]
            row += got[i, (tiles + n) * mine_n : (tiles + n + 1) * mine_n, :].astype(F32)
        part += row * block[:, n_z : n_z + 1]
        hidden[:, n * LANES : (n + 1) * LANES] = (own_grad * part).astype(BF16)
    for copy in copies:
        copy.wait()


def local(hidden, head_weight, labels, loss_grad):
    voc, feat = head_weight.shape
    mine_n = hidden.shape[0]
    n_dp = lax.axis_size("dp")
    n_sec = lax.axis_size("section")
    n_z = n_sec // 2
    half = n_z * mine_n
    tokens = 2 * half
    share = tokens // n_dp
    section = lax.axis_index("section")
    z, core = section // 2, section % 2
    j = lax.axis_index("dp")
    scalars = jnp.stack([section, z, core, j, jnp.int32(voc), jnp.int32(mine_n)]).astype(I32)
    along_z = [[2 * k + c for k in range(n_z)] for c in range(2)]
    swap = [(i, i ^ 1) for i in range(n_sec)]
    flops = 2 * tokens * voc * feat

    def exchange_z(x):
        return lax.all_to_all(x, "section", 0, 0, tiled=True, axis_index_groups=along_z)

    def exchange_dp(x):
        return lax.all_to_all(x, "dp", 0, 0, tiled=True)

    def own_core_first(x):
        x = x.reshape(n_z, 2, mine_n)
        first = jnp.where(core == 0, x[:, 0], x[:, 1])
        second = jnp.where(core == 0, x[:, 1], x[:, 0])
        return jnp.concatenate([first.reshape(half), second.reshape(half)])

    label = own_core_first(labels)
    grad = own_core_first(loss_grad)
    columns = section * voc + jnp.arange(voc, dtype=I32)

    mine = exchange_z(jnp.broadcast_to(hidden[None], (n_z, mine_n, feat))).reshape(half, feat)
    hot = label[:, None] == columns[None, :]
    rows = jnp.dot(hot.astype(BF16), head_weight, preferred_element_type=F32).astype(BF16)
    ready = (mine, rows, head_weight.T, label[None], grad[None], scalars)
    mine, rows, tall, label, grad, scalars = lax.optimization_barrier(ready)
    other = lax.ppermute(mine, "section", swap)

    width = voc + LANES
    coded, whole = call(
        logits_kernel,
        [],
        [mine, other, tall],
        [((tokens, width), I16), ((tokens, feat), BF16)],
        scratch=[((tokens, voc), F32)],
        flops=flops,
    )
    coded = exchange_dp(coded.reshape(n_dp, share, width))
    (message,) = call(
        softmax_kernel,
        [scalars, labels],
        [coded],
        [((n_dp, share, width), BF16)],
        scratch=[((share, voc), F32)],
    )
    got = exchange_dp(message).reshape(tokens, width)

    send, part, stat = call(
        partial_kernel,
        [],
        [got, head_weight],
        [((half + 16, 2 * feat), BF16), ((half, feat), F32), ((8, tokens), F32)],
        left=[rows],
        copies=1,
        flops=flops,
    )
    theirs = lax.ppermute(send, "section", swap)
    (message,) = call(
        pair_kernel,
        [scalars],
        [part, stat, theirs],
        [((n_z, (2 * feat // LANES + 1) * mine_n, LANES), BF16)],
        left=[rows],
        scratch=[((half, feat), BF16)],
        copies=1,
    )
    last = exchange_z(message)
    soft = got[:, :voc].T
    loss, grad_hidden, grad_weight = call(
        tail_kernel,
        [scalars, loss_grad],
        [last, soft, stat, whole, label, grad],
        [((1, share), F32), ((mine_n, feat), BF16), ((voc, feat), BF16)],
        scratch=[((voc, feat), BF16)],
        copies=voc // CHUNK,
        copies_out=True,
        flops=flops,
    )
    return (loss.reshape(share), grad_hidden, grad_weight)


def solution(mesh):
    return jax.shard_map(
        local,
        mesh=mesh,
        in_specs=(P("section", "dp"), P("section", "dp"), P(), P()),
        out_specs=(P("dp"), P("section", "dp"), P("section", "dp")),
        check_vma=False,
    )
```

```python
import functools

import jax
import jax.numpy as jnp
from jax import lax
from jax.experimental import pallas as pl
from jax.experimental.pallas import tpu as pltpu
from jax.sharding import PartitionSpec as P

F32 = jnp.float32
BF16 = jnp.bfloat16
I16 = jnp.int16
I32 = jnp.int32
LANES = 128
CHUNK = 256
OWN = 8
SPACE = 32
STEPS = 32760.0
GRAIN = 64.0
MIB = 1 << 20

SCALARS = pl.BlockSpec(memory_space=pltpu.SMEM)
WHOLE = pl.BlockSpec(memory_space=pltpu.VMEM)


def call(kernel, scalars, args, outs, left=(), scratch=(), copies=0, copies_out=False, flops=0):
    anywhere = pl.BlockSpec(memory_space=pl.ANY)
    out_specs = [WHOLE] * len(outs)
    scratch_shapes = [pltpu.VMEM(s, d) for s, d in scratch]
    if copies_out:
        out_specs[-1] = anywhere
    if copies:
        scratch_shapes.append(pltpu.SemaphoreType.DMA((copies,)))
    return pl.pallas_call(
        kernel,
        out_shape=[jax.ShapeDtypeStruct(s, d) for s, d in outs],
        in_specs=[SCALARS] * len(scalars) + [WHOLE] * len(args) + [anywhere] * len(left),
        out_specs=out_specs,
        scratch_shapes=scratch_shapes,
        compiler_params=pltpu.CompilerParams(vmem_limit_bytes=16 * MIB),
        cost_estimate=pl.CostEstimate(flops=flops, bytes_accessed=4 * MIB, transcendentals=0),
    )(*scalars, *args, *left)


def high_part(x):
    return x.astype(BF16).astype(F32)


def split3(x):
    a = high_part(x)
    b = high_part(x - a)
    return a, b, x - a - b


def lane_block(rows, values):
    lane = lax.broadcasted_iota(I32, (rows, LANES), 1)
    block = jnp.zeros((rows, LANES), F32)
    for k, value in enumerate(values):
        block = jnp.where(lane == k, value, block)
    return block


def join3(block, k):
    return block[k : k + 1] + block[k + 1 : k + 2] + block[k + 2 : k + 3]


def logits_kernel(mine, other, weight, out, whole, part, staged, sems):
    half = mine.shape[0]
    voc = weight.shape[0]
    starts = range(0, voc, CHUNK)
    copies = []
    for n, k in enumerate(starts):
        at = pl.ds(k, CHUNK)
        copies.append(pltpu.make_async_copy(weight.at[at], staged.at[at], sems.at[n]))
        copies[-1].start()
    whole[:half, :] = mine[...]
    whole[half:, :] = other[...]
    top = jnp.zeros((2 * half, LANES), F32)
    for copy, k in zip(copies, starts):
        copy.wait()
        block = lax.dot_general(
            whole[...],
            staged[k : k + CHUNK, :],
            (((1,), (1,)), ((), ())),
            preferred_element_type=F32,
        )
        part[:, k : k + CHUNK] = block
        size = jnp.abs(block)
        for c in range(0, CHUNK, LANES):
            top = jnp.maximum(top, size[:, c : c + LANES])
    top = jnp.max(top, axis=1, keepdims=True)
    grade = jnp.ceil(jnp.log2(jnp.maximum(top, 1e-30)) * GRAIN)
    per = STEPS * jnp.exp2(grade * (-1.0 / GRAIN))
    for k in starts:
        out[:, k : k + CHUNK] = jnp.round(part[:, k : k + CHUNK] * per).astype(I32).astype(I16)
    out[:, voc:] = jnp.broadcast_to(grade, (2 * half, LANES)).astype(I32).astype(I16)


def softmax_kernel(scalars, labels, got, out, logits):
    n, share, width = got.shape
    section, core, j, mine_n = scalars[0], scalars[2], scalars[3], scalars[5]
    voc = width - LANES
    scales = [
        jnp.exp2(got[i, :, voc:].astype(I32).astype(F32)[:, :1] * (1.0 / GRAIN)) * (1.0 / STEPS)
        for i in range(n)
    ]
    top = jnp.full((share, LANES), -jnp.inf, F32)
    for k in range(0, voc, CHUNK):
        block = jnp.zeros((share, CHUNK), F32)
        for i in range(n):
            block += got[i, :, k : k + CHUNK].astype(I32).astype(F32) * scales[i]
        logits[:, k : k + CHUNK] = block
        for c in range(0, CHUNK, LANES):
            top = jnp.maximum(top, block[:, c : c + LANES])
    top = jnp.max(top, axis=1, keepdims=True)
    total = jnp.zeros((share, CHUNK), F32)
    target = jnp.zeros((share, CHUNK), F32)
    sublane = lax.broadcasted_iota(I32, (share, 1), 0)
    place = jnp.zeros((share, 1), I32)
    for r in range(share):
        index = j * share + r
        side = index // (n * share // 2)
        index = index - side * (n * share // 2)
        first = core + side - 2 * core * side
        token = 2 * mine_n * (index // mine_n) + first * mine_n + index % mine_n
        place = jnp.where(sublane == r, labels[token], place)
    place = place - section * voc
    lane = lax.broadcasted_iota(I32, (share, CHUNK), 1)
    for k in range(0, voc, CHUNK):
        block = logits[:, k : k + CHUNK]
        expo = jnp.exp(block - top)
        total += expo
        hot = lane + k == place
        target += jnp.where(hot, block, 0.0)
        logits[:, k : k + CHUNK] = jnp.where(hot, 0.0, expo)
    total = jnp.sum(total, axis=1, keepdims=True)
    target = jnp.sum(target, axis=1, keepdims=True)
    inverse = 1.0 / total
    for k in range(0, voc, CHUNK):
        soft = (logits[:, k : k + CHUNK] * inverse).astype(BF16)
        for i in range(n):
            out[i, :, k : k + CHUNK] = soft
    stats = lane_block(share, split3(top + jnp.log(total)) + split3(target)).astype(BF16)
    for i in range(n):
        out[i, :, voc:] = stats


def send_kernel(got, weight, rows, send, stat, sems):
    voc, feat = weight.shape
    half = got.shape[0] // 2
    copy = pltpu.make_async_copy(
        rows.at[pl.ds(half, half)], send.at[pl.ds(0, half), pl.ds(feat, feat)], sems.at[0]
    )
    copy.start()
    stats = got[:, voc:].astype(F32).T[:8]
    send[half:, :LANES] = jnp.concatenate([stats[:, :half], stats[:, half:]], axis=0).astype(BF16)
    stat[...] = jnp.concatenate([join3(stats, 0), join3(stats, 3), stats[:6]], axis=0)
    send[:half, :feat] = jnp.dot(
        got[half:, :voc], weight[...], preferred_element_type=F32
    ).astype(BF16)
    copy.wait()


def keep_kernel(got, weight, part):
    voc = weight.shape[0]
    part[...] = jnp.dot(
        got[: part.shape[0], :voc], weight[...], preferred_element_type=F32
    )


def pair_kernel(scalars, part, stat, got, rows, out, own_rows, sems):
    half, feat = part.shape
    core, j, mine_n = scalars[2], scalars[3], OWN
    n_z = out.shape[0]
    copy = pltpu.make_async_copy(rows.at[pl.ds(0, half)], own_rows, sems.at[0])
    copy.start()
    theirs = got[half:, :LANES].astype(F32)
    own_log, own_target = stat[0:1, :], stat[1:2, :]
    other_log = jnp.concatenate([join3(theirs, 8), join3(theirs, 0)], axis=1)
    other_target = jnp.concatenate([join3(theirs, 11), join3(theirs, 3)], axis=1)
    first = jnp.where(core == 0, own_log, other_log)
    second = jnp.where(core == 0, other_log, own_log)
    top = jnp.maximum(first, second)
    pair_log = top + jnp.log(jnp.exp(first - top) + jnp.exp(second - top))
    shares = jnp.concatenate(
        [jnp.exp(own_log - pair_log)[:, :half], jnp.exp(other_log - pair_log)[:, :half]], axis=0
    )
    shares = jnp.concatenate([shares] * (half // 2), axis=0).T
    total = part[...] * shares[:, 0:1] + got[:half, :feat].astype(F32) * shares[:, 1:2]
    logs = split3(pair_log)
    logs = [x[:, h * half : (h + 1) * half] for h in range(2) for x in logs]
    targets = jnp.concatenate(split3(own_target + other_target), axis=0)
    targets = jnp.concatenate([targets] * 3, axis=0)[:8]
    mine, other = targets[:, :half], targets[:, half:]
    lane = lax.broadcasted_iota(I32, (1, half), 1)
    base = jnp.zeros((1, half), F32)
    for k in range(3):
        for n, x in enumerate((mine, other)):
            at = SPACE * k + (n + 1) * mine_n
            moved = pltpu.roll(x, (half + at - mine_n * j) % half, 1)[k : k + 1]
            base = jnp.where((lane >= at) & (lane < at + mine_n), moved, base)
    copy.wait()
    label_rows = own_rows[...].astype(F32) + got[:half, feat:].astype(F32)
    for i in range(n_z):
        row = base
        for k in range(3):
            at = SPACE * k
            moved = pltpu.roll(mine, (half + at - mine_n * i) % half, 1)[k : k + 1]
            row = jnp.where((lane >= at) & (lane < at + mine_n), moved, row)
        at = slice(i * mine_n, (i + 1) * mine_n)
        for n, k in enumerate(range(0, feat, LANES)):
            here = slice(n * mine_n, (n + 1) * mine_n)
            out[i, here, :] = total[at, k : k + LANES].astype(BF16)
            here = slice(here.start + feat // LANES * mine_n, here.stop + feat // LANES * mine_n)
            out[i, here, :] = label_rows[at, k : k + LANES].astype(BF16)
        out[i, here.stop :, :] = jnp.concatenate(logs + [row, row], axis=0).astype(BF16)


def tail_kernel(
    scalars,
    loss_grad,
    got,
    soft,
    stat,
    whole,
    label,
    grad,
    loss,
    hidden,
    weight,
    staged,
    sems,
):
    n_z, mine_n = got.shape[0], hidden.shape[0]
    tokens, feat = whole.shape
    tiles = feat // LANES
    half = tokens // 2
    section, z, core = scalars[0], scalars[1], scalars[2]
    j, voc = scalars[3], scalars[4]
    pieces = [got[:, 2 * tiles * mine_n + k, :].astype(F32) for k in range(7)]
    logs = jnp.concatenate(
        [pieces[0] + pieces[1] + pieces[2], pieces[3] + pieces[4] + pieces[5]], axis=1
    )
    top = jnp.max(logs, axis=0, keepdims=True)
    log_total = top + jnp.log(jnp.sum(jnp.exp(logs - top), axis=0, keepdims=True))

    scale = grad[...] * jnp.exp(stat[0:1, :] - log_total)
    label_grad = grad[...] * (jnp.exp(stat[1:2, :] - log_total) - 1.0)
    place = label[...] - section * voc
    line = lax.broadcasted_iota(I32, (CHUNK, tokens), 0)
    copies = []
    for n, k in enumerate(range(0, weight.shape[0], CHUNK)):
        value = soft[k : k + CHUNK, :].astype(F32) * scale
        value = jnp.where(line + k == place, label_grad, value).astype(BF16)
        staged[k : k + CHUNK, :] = jnp.dot(
            value, whole[...], preferred_element_type=F32
        ).astype(BF16)
        at = pl.ds(k, CHUNK)
        copies.append(pltpu.make_async_copy(staged.at[at], weight.at[at], sems.at[n]))
        copies[-1].start()

    target = (
        pieces[6]
        + pltpu.roll(pieces[6], half - SPACE, 1)
        + pltpu.roll(pieces[6], half - 2 * SPACE, 1)
    )
    target = jnp.broadcast_to(jnp.sum(target, axis=0, keepdims=True), (8, half))
    lane = lax.broadcasted_iota(I32, (8, half), 1)
    mine, other = (
        jnp.broadcast_to(x, (8, half)) for x in (log_total[:, :half], log_total[:, half:])
    )
    first = pltpu.roll(mine, (half - mine_n * j) % half, 1) - pltpu.roll(target, half - mine_n, 1)
    second = pltpu.roll(other, (half - mine_n * j) % half, 1) - pltpu.roll(
        target, half - 2 * mine_n, 1
    )
    low = jnp.where(core == 0, first, second)
    high = pltpu.roll(jnp.where(core == 0, second, first), mine_n, 1)
    loss[...] = jnp.where(lane < mine_n, low, high)[:1, : loss.shape[1]]

    back = (half - mine_n * z) % half
    shares = pltpu.roll(jnp.exp(logs[:, :half] - log_total[:, :half]), back, 1)
    label_part = jnp.exp(target - pltpu.roll(mine, back, 1)) - 1.0
    block = [shares] + [label_part] * ((half - n_z) // 8)
    block = jnp.concatenate(block, axis=0).T[:mine_n]
    sublane = lax.broadcasted_iota(I32, (mine_n, 1), 0)
    own_grad = jnp.zeros((mine_n, 1), F32)
    for r in range(mine_n):
        own_grad = jnp.where(sublane == r, loss_grad[section * mine_n + r], own_grad)
    for n in range(tiles):
        part = jnp.zeros((mine_n, LANES), F32)
        row = jnp.zeros((mine_n, LANES), F32)
        for i in range(n_z):
            part += got[i, n * mine_n : (n + 1) * mine_n, :].astype(F32) * block[:, i : i + 1]
            row += got[i, (tiles + n) * mine_n : (tiles + n + 1) * mine_n, :].astype(F32)
        part += row * block[:, n_z : n_z + 1]
        hidden[:, n * LANES : (n + 1) * LANES] = (own_grad * part).astype(BF16)
    for copy in copies:
        copy.wait()


def local(hidden, head_weight, labels, loss_grad):
    voc, feat = head_weight.shape
    mine_n = hidden.shape[0]
    n_dp = lax.axis_size("dp")
    n_sec = lax.axis_size("section")
    n_z = n_sec // 2
    half = n_z * mine_n
    tokens = 2 * half
    share = tokens // n_dp
    section = lax.axis_index("section")
    z, core = section // 2, section % 2
    j = lax.axis_index("dp")
    scalars = jnp.stack([section, z, core, j, jnp.int32(voc), jnp.int32(mine_n)]).astype(I32)
    along_z = [[2 * k + c for k in range(n_z)] for c in range(2)]
    swap = [(i, i ^ 1) for i in range(n_sec)]
    flops = 2 * tokens * voc * feat

    def exchange_z(x):
        return lax.all_to_all(x, "section", 0, 0, tiled=True, axis_index_groups=along_z)

    def exchange_dp(x):
        return lax.all_to_all(x, "dp", 0, 0, tiled=True)

    def own_core_first(x):
        x = x.reshape(n_z, 2, mine_n)
        first = jnp.where(core == 0, x[:, 0], x[:, 1])
        second = jnp.where(core == 0, x[:, 1], x[:, 0])
        return jnp.concatenate([first.reshape(half), second.reshape(half)])

    columns = section * voc + jnp.arange(voc, dtype=I32)

    mine = exchange_z(jnp.broadcast_to(hidden[None], (n_z, mine_n, feat))).reshape(half, feat)
    hot = own_core_first(labels)[:, None] == columns[None, :]
    rows = jnp.dot(hot.astype(BF16), head_weight, preferred_element_type=F32).astype(BF16)
    mine, rows, scalars = lax.optimization_barrier((mine, rows, scalars))
    other = lax.ppermute(mine, "section", swap)

    width = voc + LANES
    coded, whole = call(
        logits_kernel,
        [],
        [mine, other],
        [((tokens, width), I16), ((tokens, feat), BF16)],
        left=[head_weight],
        scratch=[((tokens, voc), F32), ((voc, feat), BF16)],
        copies=voc // CHUNK,
        flops=flops,
    )
    coded = exchange_dp(coded.reshape(n_dp, share, width))
    (message,) = call(
        softmax_kernel,
        [scalars, labels],
        [coded],
        [((n_dp, share, width), BF16)],
        scratch=[((share, voc), F32)],
    )
    got = exchange_dp(message).reshape(tokens, width)

    send, stat = call(
        send_kernel,
        [],
        [got, head_weight],
        [((half + 16, 2 * feat), BF16), ((8, tokens), F32)],
        left=[rows],
        copies=1,
        flops=flops // 2,
    )
    theirs = lax.ppermute(send, "section", swap)
    (part,) = call(keep_kernel, [], [got, head_weight], [((half, feat), F32)], flops=flops // 2)
    (message,) = call(
        pair_kernel,
        [scalars],
        [part, stat, theirs],
        [((n_z, (2 * feat // LANES + 1) * mine_n, LANES), BF16)],
        left=[rows],
        scratch=[((half, feat), BF16)],
        copies=1,
    )
    last = exchange_z(message)
    soft = got[:, :voc].T
    late = lax.optimization_barrier((labels, loss_grad, message))
    label, grad = own_core_first(late[0])[None], own_core_first(late[1])[None]
    loss, grad_hidden, grad_weight = call(
        tail_kernel,
        [scalars, loss_grad],
        [last, soft, stat, whole, label, grad],
        [((1, share), F32), ((mine_n, feat), BF16), ((voc, feat), BF16)],
        scratch=[((voc, feat), BF16)],
        copies=voc // CHUNK,
        copies_out=True,
        flops=flops,
    )
    return (loss.reshape(share), grad_hidden, grad_weight)


def solution(mesh):
    return jax.shard_map(
        local,
        mesh=mesh,
        in_specs=(P("section", "dp"), P("section", "dp"), P(), P()),
        out_specs=(P("dp"), P("section", "dp"), P("section", "dp")),
        check_vma=False,
    )
```

```python
import functools

import jax
import jax.numpy as jnp
from jax import lax
from jax.experimental import pallas as pl
from jax.experimental.pallas import tpu as pltpu
from jax.sharding import PartitionSpec as P

F32 = jnp.float32
BF16 = jnp.bfloat16
I16 = jnp.int16
I32 = jnp.int32
LANES = 128
CHUNK = 256
OWN = 8
SPACE = 32
STEPS = 32760.0
GRAIN = 64.0
MIB = 1 << 20

SCALARS = pl.BlockSpec(memory_space=pltpu.SMEM)
WHOLE = pl.BlockSpec(memory_space=pltpu.VMEM)


def call(kernel, scalars, args, outs, left=(), scratch=(), copies=0, copies_out=False, flops=0):
    anywhere = pl.BlockSpec(memory_space=pl.ANY)
    out_specs = [WHOLE] * len(outs)
    scratch_shapes = [pltpu.VMEM(s, d) for s, d in scratch]
    if copies_out:
        out_specs[-1] = anywhere
    if copies:
        scratch_shapes.append(pltpu.SemaphoreType.DMA((copies,)))
    return pl.pallas_call(
        kernel,
        out_shape=[jax.ShapeDtypeStruct(s, d) for s, d in outs],
        in_specs=[SCALARS] * len(scalars) + [WHOLE] * len(args) + [anywhere] * len(left),
        out_specs=out_specs,
        scratch_shapes=scratch_shapes,
        compiler_params=pltpu.CompilerParams(vmem_limit_bytes=16 * MIB),
        cost_estimate=pl.CostEstimate(flops=flops, bytes_accessed=4 * MIB, transcendentals=0),
    )(*scalars, *args, *left)


def high_part(x):
    return x.astype(BF16).astype(F32)


def split3(x):
    a = high_part(x)
    b = high_part(x - a)
    return a, b, x - a - b


def lane_block(rows, values):
    lane = lax.broadcasted_iota(I32, (rows, LANES), 1)
    block = jnp.zeros((rows, LANES), F32)
    for k, value in enumerate(values):
        block = jnp.where(lane == k, value, block)
    return block


def join3(block, k):
    return block[k : k + 1] + block[k + 1 : k + 2] + block[k + 2 : k + 3]


def prepare_kernel(weight, label, tall, rows):
    voc, feat = weight.shape
    tokens = label.shape[0]
    lane = lax.broadcasted_iota(I32, (tokens, CHUNK), 1)
    total = jnp.zeros((tokens, feat), F32)
    for k in range(0, voc, CHUNK):
        block = weight[k : k + CHUNK, :]
        tall[:, k : k + CHUNK] = block.T
        hot = (lane + k == label[...]).astype(BF16)
        total += jnp.dot(hot, block, preferred_element_type=F32)
    rows[...] = total.astype(BF16)


def logits_kernel(mine, other, weight, out, whole, part):
    half = mine.shape[0]
    voc = weight.shape[1]
    whole[:half, :] = mine[...]
    whole[half:, :] = other[...]
    top = jnp.zeros((2 * half, LANES), F32)
    for k in range(0, voc, CHUNK):
        block = jnp.dot(whole[...], weight[:, k : k + CHUNK], preferred_element_type=F32)
        part[:, k : k + CHUNK] = block
        size = jnp.abs(block)
        for c in range(0, CHUNK, LANES):
            top = jnp.maximum(top, size[:, c : c + LANES])
    top = jnp.max(top, axis=1, keepdims=True)
    grade = jnp.ceil(jnp.log2(jnp.maximum(top, 1e-30)) * GRAIN)
    per = STEPS * jnp.exp2(grade * (-1.0 / GRAIN))
    for k in range(0, voc, CHUNK):
        out[:, k : k + CHUNK] = jnp.round(part[:, k : k + CHUNK] * per).astype(I32).astype(I16)
    out[:, voc:] = jnp.broadcast_to(grade, (2 * half, LANES)).astype(I32).astype(I16)


def softmax_kernel(scalars, labels, got, out, logits):
    n, share, width = got.shape
    section, core, j, mine_n = scalars[0], scalars[2], scalars[3], scalars[5]
    voc = width - LANES
    scales = [
        jnp.exp2(got[i, :, voc:].astype(I32).astype(F32)[:, :1] * (1.0 / GRAIN)) * (1.0 / STEPS)
        for i in range(n)
    ]
    top = jnp.full((share, LANES), -jnp.inf, F32)
    for k in range(0, voc, CHUNK):
        block = jnp.zeros((share, CHUNK), F32)
        for i in range(n):
            block += got[i, :, k : k + CHUNK].astype(I32).astype(F32) * scales[i]
        logits[:, k : k + CHUNK] = block
        for c in range(0, CHUNK, LANES):
            top = jnp.maximum(top, block[:, c : c + LANES])
    top = jnp.max(top, axis=1, keepdims=True)
    total = jnp.zeros((share, CHUNK), F32)
    target = jnp.zeros((share, CHUNK), F32)
    sublane = lax.broadcasted_iota(I32, (share, 1), 0)
    place = jnp.zeros((share, 1), I32)
    for r in range(share):
        index = j * share + r
        side = index // (n * share // 2)
        index = index - side * (n * share // 2)
        first = core + side - 2 * core * side
        token = 2 * mine_n * (index // mine_n) + first * mine_n + index % mine_n
        place = jnp.where(sublane == r, labels[token], place)
    place = place - section * voc
    lane = lax.broadcasted_iota(I32, (share, CHUNK), 1)
    for k in range(0, voc, CHUNK):
        block = logits[:, k : k + CHUNK]
        expo = jnp.exp(block - top)
        total += expo
        hot = lane + k == place
        target += jnp.where(hot, block, 0.0)
        logits[:, k : k + CHUNK] = jnp.where(hot, 0.0, expo)
    total = jnp.sum(total, axis=1, keepdims=True)
    target = jnp.sum(target, axis=1, keepdims=True)
    inverse = 1.0 / total
    for k in range(0, voc, CHUNK):
        soft = (logits[:, k : k + CHUNK] * inverse).astype(BF16)
        for i in range(n):
            out[i, :, k : k + CHUNK] = soft
    stats = lane_block(share, split3(top + jnp.log(total)) + split3(target)).astype(BF16)
    for i in range(n):
        out[i, :, voc:] = stats


def send_kernel(got, weight, rows, send, stat, sems):
    voc, feat = weight.shape
    half = got.shape[0] // 2
    copy = pltpu.make_async_copy(
        rows.at[pl.ds(half, half)], send.at[pl.ds(0, half), pl.ds(feat, feat)], sems.at[0]
    )
    copy.start()
    stats = got[:, voc:].astype(F32).T[:8]
    send[half:, :LANES] = jnp.concatenate([stats[:, :half], stats[:, half:]], axis=0).astype(BF16)
    stat[...] = jnp.concatenate([join3(stats, 0), join3(stats, 3), stats[:6]], axis=0)
    send[:half, :feat] = jnp.dot(
        got[half:, :voc], weight[...], preferred_element_type=F32
    ).astype(BF16)
    copy.wait()


def keep_kernel(got, weight, part):
    voc = weight.shape[0]
    part[...] = jnp.dot(
        got[: part.shape[0], :voc], weight[...], preferred_element_type=F32
    )


def pair_kernel(scalars, part, stat, got, rows, out, own_rows, sems):
    half, feat = part.shape
    core, j, mine_n = scalars[2], scalars[3], OWN
    n_z = out.shape[0]
    copy = pltpu.make_async_copy(rows.at[pl.ds(0, half)], own_rows, sems.at[0])
    copy.start()
    theirs = got[half:, :LANES].astype(F32)
    own_log, own_target = stat[0:1, :], stat[1:2, :]
    other_log = jnp.concatenate([join3(theirs, 8), join3(theirs, 0)], axis=1)
    other_target = jnp.concatenate([join3(theirs, 11), join3(theirs, 3)], axis=1)
    first = jnp.where(core == 0, own_log, other_log)
    second = jnp.where(core == 0, other_log, own_log)
    top = jnp.maximum(first, second)
    pair_log = top + jnp.log(jnp.exp(first - top) + jnp.exp(second - top))
    shares = jnp.concatenate(
        [jnp.exp(own_log - pair_log)[:, :half], jnp.exp(other_log - pair_log)[:, :half]], axis=0
    )
    shares = jnp.concatenate([shares] * (half // 2), axis=0).T
    total = part[...] * shares[:, 0:1] + got[:half, :feat].astype(F32) * shares[:, 1:2]
    logs = split3(pair_log)
    logs = [x[:, h * half : (h + 1) * half] for h in range(2) for x in logs]
    targets = jnp.concatenate(split3(own_target + other_target), axis=0)
    targets = jnp.concatenate([targets] * 3, axis=0)[:8]
    mine, other = targets[:, :half], targets[:, half:]
    lane = lax.broadcasted_iota(I32, (1, half), 1)
    base = jnp.zeros((1, half), F32)
    for k in range(3):
        for n, x in enumerate((mine, other)):
            at = SPACE * k + (n + 1) * mine_n
            moved = pltpu.roll(x, (half + at - mine_n * j) % half, 1)[k : k + 1]
            base = jnp.where((lane >= at) & (lane < at + mine_n), moved, base)
    copy.wait()
    label_rows = own_rows[...].astype(F32) + got[:half, feat:].astype(F32)
    for i in range(n_z):
        row = base
        for k in range(3):
            at = SPACE * k
            moved = pltpu.roll(mine, (half + at - mine_n * i) % half, 1)[k : k + 1]
            row = jnp.where((lane >= at) & (lane < at + mine_n), moved, row)
        at = slice(i * mine_n, (i + 1) * mine_n)
        for n, k in enumerate(range(0, feat, LANES)):
            here = slice(n * mine_n, (n + 1) * mine_n)
            out[i, here, :] = total[at, k : k + LANES].astype(BF16)
            here = slice(here.start + feat // LANES * mine_n, here.stop + feat // LANES * mine_n)
            out[i, here, :] = label_rows[at, k : k + LANES].astype(BF16)
        out[i, here.stop :, :] = jnp.concatenate(logs + [row, row], axis=0).astype(BF16)


def tail_kernel(
    scalars,
    loss_grad,
    got,
    soft,
    stat,
    whole,
    label,
    grad,
    loss,
    hidden,
    weight,
    staged,
    sems,
):
    n_z, mine_n = got.shape[0], hidden.shape[0]
    tokens, feat = whole.shape
    tiles = feat // LANES
    half = tokens // 2
    section, z, core = scalars[0], scalars[1], scalars[2]
    j, voc = scalars[3], scalars[4]
    pieces = [got[:, 2 * tiles * mine_n + k, :].astype(F32) for k in range(7)]
    logs = jnp.concatenate(
        [pieces[0] + pieces[1] + pieces[2], pieces[3] + pieces[4] + pieces[5]], axis=1
    )
    top = jnp.max(logs, axis=0, keepdims=True)
    log_total = top + jnp.log(jnp.sum(jnp.exp(logs - top), axis=0, keepdims=True))

    scale = grad[...] * jnp.exp(stat[0:1, :] - log_total)
    label_grad = grad[...] * (jnp.exp(stat[1:2, :] - log_total) - 1.0)
    place = label[...] - section * voc
    line = lax.broadcasted_iota(I32, (CHUNK, tokens), 0)
    copies = []
    for n, k in enumerate(range(0, weight.shape[0], CHUNK)):
        value = soft[k : k + CHUNK, :].astype(F32) * scale
        value = jnp.where(line + k == place, label_grad, value).astype(BF16)
        staged[k : k + CHUNK, :] = jnp.dot(
            value, whole[...], preferred_element_type=F32
        ).astype(BF16)
        at = pl.ds(k, CHUNK)
        copies.append(pltpu.make_async_copy(staged.at[at], weight.at[at], sems.at[n]))
        copies[-1].start()

    target = (
        pieces[6]
        + pltpu.roll(pieces[6], half - SPACE, 1)
        + pltpu.roll(pieces[6], half - 2 * SPACE, 1)
    )
    target = jnp.broadcast_to(jnp.sum(target, axis=0, keepdims=True), (8, half))
    lane = lax.broadcasted_iota(I32, (8, half), 1)
    mine, other = (
        jnp.broadcast_to(x, (8, half)) for x in (log_total[:, :half], log_total[:, half:])
    )
    first = pltpu.roll(mine, (half - mine_n * j) % half, 1) - pltpu.roll(target, half - mine_n, 1)
    second = pltpu.roll(other, (half - mine_n * j) % half, 1) - pltpu.roll(
        target, half - 2 * mine_n, 1
    )
    low = jnp.where(core == 0, first, second)
    high = pltpu.roll(jnp.where(core == 0, second, first), mine_n, 1)
    loss[...] = jnp.where(lane < mine_n, low, high)[:1, : loss.shape[1]]

    back = (half - mine_n * z) % half
    shares = pltpu.roll(jnp.exp(logs[:, :half] - log_total[:, :half]), back, 1)
    label_part = jnp.exp(target - pltpu.roll(mine, back, 1)) - 1.0
    block = [shares] + [label_part] * ((half - n_z) // 8)
    block = jnp.concatenate(block, axis=0).T[:mine_n]
    sublane = lax.broadcasted_iota(I32, (mine_n, 1), 0)
    own_grad = jnp.zeros((mine_n, 1), F32)
    for r in range(mine_n):
        own_grad = jnp.where(sublane == r, loss_grad[section * mine_n + r], own_grad)
    for n in range(tiles):
        part = jnp.zeros((mine_n, LANES), F32)
        row = jnp.zeros((mine_n, LANES), F32)
        for i in range(n_z):
            part += got[i, n * mine_n : (n + 1) * mine_n, :].astype(F32) * block[:, i : i + 1]
            row += got[i, (tiles + n) * mine_n : (tiles + n + 1) * mine_n, :].astype(F32)
        part += row * block[:, n_z : n_z + 1]
        hidden[:, n * LANES : (n + 1) * LANES] = (own_grad * part).astype(BF16)
    for copy in copies:
        copy.wait()


def local(hidden, head_weight, labels, loss_grad):
    voc, feat = head_weight.shape
    mine_n = hidden.shape[0]
    n_dp = lax.axis_size("dp")
    n_sec = lax.axis_size("section")
    n_z = n_sec // 2
    half = n_z * mine_n
    tokens = 2 * half
    share = tokens // n_dp
    section = lax.axis_index("section")
    z, core = section // 2, section % 2
    j = lax.axis_index("dp")
    scalars = jnp.stack([section, z, core, j, jnp.int32(voc), jnp.int32(mine_n)]).astype(I32)
    along_z = [[2 * k + c for k in range(n_z)] for c in range(2)]
    swap = [(i, i ^ 1) for i in range(n_sec)]
    flops = 2 * tokens * voc * feat

    def exchange_z(x):
        return lax.all_to_all(x, "section", 0, 0, tiled=True, axis_index_groups=along_z)

    def exchange_dp(x):
        return lax.all_to_all(x, "dp", 0, 0, tiled=True)

    def own_core_first(x):
        x = x.reshape(n_z, 2, mine_n)
        first = jnp.where(core == 0, x[:, 0], x[:, 1])
        second = jnp.where(core == 0, x[:, 1], x[:, 0])
        return jnp.concatenate([first.reshape(half), second.reshape(half)])

    mine = exchange_z(jnp.broadcast_to(hidden[None], (n_z, mine_n, feat))).reshape(half, feat)
    tall, rows = call(
        prepare_kernel,
        [],
        [head_weight, (own_core_first(labels) - section * voc)[:, None]],
        [((feat, voc), BF16), ((tokens, feat), BF16)],
        flops=flops,
    )
    mine, tall, rows, scalars = lax.optimization_barrier((mine, tall, rows, scalars))
    other = lax.ppermute(mine, "section", swap)

    width = voc + LANES
    coded, whole = call(
        logits_kernel,
        [],
        [mine, other, tall],
        [((tokens, width), I16), ((tokens, feat), BF16)],
        scratch=[((tokens, voc), F32)],
        flops=flops,
    )
    coded = exchange_dp(coded.reshape(n_dp, share, width))
    (message,) = call(
        softmax_kernel,
        [scalars, labels],
        [coded],
        [((n_dp, share, width), BF16)],
        scratch=[((share, voc), F32)],
    )
    got = exchange_dp(message).reshape(tokens, width)

    send, stat = call(
        send_kernel,
        [],
        [got, head_weight],
        [((half + 16, 2 * feat), BF16), ((8, tokens), F32)],
        left=[rows],
        copies=1,
        flops=flops // 2,
    )
    theirs = lax.ppermute(send, "section", swap)
    (part,) = call(keep_kernel, [], [got, head_weight], [((half, feat), F32)], flops=flops // 2)
    (message,) = call(
        pair_kernel,
        [scalars],
        [part, stat, theirs],
        [((n_z, (2 * feat // LANES + 1) * mine_n, LANES), BF16)],
        left=[rows],
        scratch=[((half, feat), BF16)],
        copies=1,
    )
    last = exchange_z(message)
    soft = got[:, :voc].T
    late = lax.optimization_barrier((labels, loss_grad, message))
    label, grad = own_core_first(late[0])[None], own_core_first(late[1])[None]
    loss, grad_hidden, grad_weight = call(
        tail_kernel,
        [scalars, loss_grad],
        [last, soft, stat, whole, label, grad],
        [((1, share), F32), ((mine_n, feat), BF16), ((voc, feat), BF16)],
        scratch=[((voc, feat), BF16)],
        copies=voc // CHUNK,
        copies_out=True,
        flops=flops,
    )
    return (loss.reshape(share), grad_hidden, grad_weight)


def solution(mesh):
    return jax.shard_map(
        local,
        mesh=mesh,
        in_specs=(P("section", "dp"), P("section", "dp"), P(), P()),
        out_specs=(P("dp"), P("section", "dp"), P("section", "dp")),
        check_vma=False,
    )
```

```python
import functools

import jax
import jax.numpy as jnp
from jax import lax
from jax.experimental import pallas as pl
from jax.experimental.pallas import tpu as pltpu
from jax.sharding import PartitionSpec as P

F32 = jnp.float32
BF16 = jnp.bfloat16
I16 = jnp.int16
I32 = jnp.int32
LANES = 128
CHUNK = 256
OWN = 8
SPACE = 32
STEPS = 32760.0
GRAIN = 64.0
MIB = 1 << 20

SCALARS = pl.BlockSpec(memory_space=pltpu.SMEM)
WHOLE = pl.BlockSpec(memory_space=pltpu.VMEM)


def call(kernel, scalars, args, outs, left=(), scratch=(), copies=0, copies_out=False, flops=0):
    anywhere = pl.BlockSpec(memory_space=pl.ANY)
    out_specs = [WHOLE] * len(outs)
    scratch_shapes = [pltpu.VMEM(s, d) for s, d in scratch]
    if copies_out:
        out_specs[-1] = anywhere
    if copies:
        scratch_shapes.append(pltpu.SemaphoreType.DMA((copies,)))
    return pl.pallas_call(
        kernel,
        out_shape=[jax.ShapeDtypeStruct(s, d) for s, d in outs],
        in_specs=[SCALARS] * len(scalars) + [WHOLE] * len(args) + [anywhere] * len(left),
        out_specs=out_specs,
        scratch_shapes=scratch_shapes,
        compiler_params=pltpu.CompilerParams(vmem_limit_bytes=16 * MIB),
        cost_estimate=pl.CostEstimate(flops=flops, bytes_accessed=4 * MIB, transcendentals=0),
    )(*scalars, *args, *left)


def high_part(x):
    return x.astype(BF16).astype(F32)


def split3(x):
    a = high_part(x)
    b = high_part(x - a)
    return a, b, x - a - b


def lane_block(rows, values):
    lane = lax.broadcasted_iota(I32, (rows, LANES), 1)
    block = jnp.zeros((rows, LANES), F32)
    for k, value in enumerate(values):
        block = jnp.where(lane == k, value, block)
    return block


def join3(block, k):
    return block[k : k + 1] + block[k + 1 : k + 2] + block[k + 2 : k + 3]


def prepare_kernel(weight, label, tall, rows):
    voc, feat = weight.shape
    tokens = label.shape[0]
    lane = lax.broadcasted_iota(I32, (tokens, CHUNK), 1)
    total = jnp.zeros((tokens, feat), F32)
    for k in range(0, voc, CHUNK):
        block = weight[k : k + CHUNK, :]
        tall[:, k : k + CHUNK] = block.T
        hot = (lane + k == label[...]).astype(BF16)
        total += jnp.dot(hot, block, preferred_element_type=F32)
    rows[...] = total.astype(BF16)


def code_logits(tokens, weight, out, part, first):
    count = tokens.shape[0]
    rows = slice(first, first + count)
    voc = weight.shape[1]
    top = jnp.zeros((count, LANES), F32)
    for k in range(0, voc, CHUNK):
        block = jnp.dot(tokens[...], weight[:, k : k + CHUNK], preferred_element_type=F32)
        part[:, k : k + CHUNK] = block
        size = jnp.abs(block)
        for c in range(0, CHUNK, LANES):
            top = jnp.maximum(top, size[:, c : c + LANES])
    top = jnp.max(top, axis=1, keepdims=True)
    grade = jnp.ceil(jnp.log2(jnp.maximum(top, 1e-30)) * GRAIN)
    per = STEPS * jnp.exp2(grade * (-1.0 / GRAIN))
    for k in range(0, voc, CHUNK):
        out[rows, k : k + CHUNK] = (
            jnp.round(part[:, k : k + CHUNK] * per).astype(I32).astype(I16)
        )
    out[rows, voc:] = jnp.broadcast_to(grade, (count, LANES)).astype(I32).astype(I16)


def mine_kernel(mine, weight, out, part):
    code_logits(mine, weight, out, part, 0)


def other_kernel(coded, mine, other, weight, out, whole, part):
    half = mine.shape[0]
    out[:half, :] = coded[...]
    whole[:half, :] = mine[...]
    whole[half:, :] = other[...]
    code_logits(other, weight, out, part, half)


def softmax_kernel(scalars, labels, got, out, logits):
    n, share, width = got.shape
    section, core, j, mine_n = scalars[0], scalars[2], scalars[3], scalars[5]
    voc = width - LANES
    scales = [
        jnp.exp2(got[i, :, voc:].astype(I32).astype(F32)[:, :1] * (1.0 / GRAIN)) * (1.0 / STEPS)
        for i in range(n)
    ]
    top = jnp.full((share, LANES), -jnp.inf, F32)
    for k in range(0, voc, CHUNK):
        block = jnp.zeros((share, CHUNK), F32)
        for i in range(n):
            block += got[i, :, k : k + CHUNK].astype(I32).astype(F32) * scales[i]
        logits[:, k : k + CHUNK] = block
        for c in range(0, CHUNK, LANES):
            top = jnp.maximum(top, block[:, c : c + LANES])
    top = jnp.max(top, axis=1, keepdims=True)
    total = jnp.zeros((share, CHUNK), F32)
    target = jnp.zeros((share, CHUNK), F32)
    sublane = lax.broadcasted_iota(I32, (share, 1), 0)
    place = jnp.zeros((share, 1), I32)
    for r in range(share):
        index = j * share + r
        side = index // (n * share // 2)
        index = index - side * (n * share // 2)
        first = core + side - 2 * core * side
        token = 2 * mine_n * (index // mine_n) + first * mine_n + index % mine_n
        place = jnp.where(sublane == r, labels[token], place)
    place = place - section * voc
    lane = lax.broadcasted_iota(I32, (share, CHUNK), 1)
    for k in range(0, voc, CHUNK):
        block = logits[:, k : k + CHUNK]
        expo = jnp.exp(block - top)
        total += expo
        hot = lane + k == place
        target += jnp.where(hot, block, 0.0)
        logits[:, k : k + CHUNK] = jnp.where(hot, 0.0, expo)
    total = jnp.sum(total, axis=1, keepdims=True)
    target = jnp.sum(target, axis=1, keepdims=True)
    inverse = 1.0 / total
    for k in range(0, voc, CHUNK):
        soft = (logits[:, k : k + CHUNK] * inverse).astype(BF16)
        for i in range(n):
            out[i, :, k : k + CHUNK] = soft
    stats = lane_block(share, split3(top + jnp.log(total)) + split3(target)).astype(BF16)
    for i in range(n):
        out[i, :, voc:] = stats


def send_kernel(got, weight, send, stat):
    voc = weight.shape[0]
    half = got.shape[0] // 2
    stats = got[:, voc:].astype(F32).T[:8]
    send[half:, :LANES] = jnp.concatenate([stats[:, :half], stats[:, half:]], axis=0).astype(BF16)
    stat[...] = jnp.concatenate([join3(stats, 0), join3(stats, 3), stats[:6]], axis=0)
    send[:half, :] = jnp.dot(
        got[half:, :voc], weight[...], preferred_element_type=F32
    ).astype(BF16)


def keep_kernel(got, weight, part):
    voc = weight.shape[0]
    part[...] = jnp.dot(
        got[: part.shape[0], :voc], weight[...], preferred_element_type=F32
    )


def pair_kernel(scalars, part, stat, got, label_rows, out):
    half, feat = part.shape
    core, j, mine_n = scalars[2], scalars[3], OWN
    n_z = out.shape[0]
    theirs = got[half:, :LANES].astype(F32)
    own_log, own_target = stat[0:1, :], stat[1:2, :]
    other_log = jnp.concatenate([join3(theirs, 8), join3(theirs, 0)], axis=1)
    other_target = jnp.concatenate([join3(theirs, 11), join3(theirs, 3)], axis=1)
    first = jnp.where(core == 0, own_log, other_log)
    second = jnp.where(core == 0, other_log, own_log)
    top = jnp.maximum(first, second)
    pair_log = top + jnp.log(jnp.exp(first - top) + jnp.exp(second - top))
    shares = jnp.concatenate(
        [jnp.exp(own_log - pair_log)[:, :half], jnp.exp(other_log - pair_log)[:, :half]], axis=0
    )
    shares = jnp.concatenate([shares] * (half // 2), axis=0).T
    total = part[...] * shares[:, 0:1] + got[:half, :].astype(F32) * shares[:, 1:2]
    logs = split3(pair_log)
    logs = [x[:, h * half : (h + 1) * half] for h in range(2) for x in logs]
    targets = jnp.concatenate(split3(own_target + other_target), axis=0)
    targets = jnp.concatenate([targets] * 3, axis=0)[:8]
    mine, other = targets[:, :half], targets[:, half:]
    lane = lax.broadcasted_iota(I32, (1, half), 1)
    base = jnp.zeros((1, half), F32)
    for k in range(3):
        for n, x in enumerate((mine, other)):
            at = SPACE * k + (n + 1) * mine_n
            moved = pltpu.roll(x, (half + at - mine_n * j) % half, 1)[k : k + 1]
            base = jnp.where((lane >= at) & (lane < at + mine_n), moved, base)
    for i in range(n_z):
        row = base
        for k in range(3):
            at = SPACE * k
            moved = pltpu.roll(mine, (half + at - mine_n * i) % half, 1)[k : k + 1]
            row = jnp.where((lane >= at) & (lane < at + mine_n), moved, row)
        at = slice(i * mine_n, (i + 1) * mine_n)
        for n, k in enumerate(range(0, feat, LANES)):
            here = slice(n * mine_n, (n + 1) * mine_n)
            out[i, here, :] = total[at, k : k + LANES].astype(BF16)
            here = slice(here.start + feat // LANES * mine_n, here.stop + feat // LANES * mine_n)
            out[i, here, :] = label_rows[at, k : k + LANES]
        out[i, here.stop :, :] = jnp.concatenate(logs + [row, row], axis=0).astype(BF16)


def tail_kernel(
    scalars,
    loss_grad,
    got,
    soft,
    stat,
    whole,
    label,
    grad,
    loss,
    hidden,
    weight,
    staged,
    sems,
):
    n_z, mine_n = got.shape[0], hidden.shape[0]
    tokens, feat = whole.shape
    tiles = feat // LANES
    half = tokens // 2
    section, z, core = scalars[0], scalars[1], scalars[2]
    j, voc = scalars[3], scalars[4]
    pieces = [got[:, 2 * tiles * mine_n + k, :].astype(F32) for k in range(7)]
    logs = jnp.concatenate(
        [pieces[0] + pieces[1] + pieces[2], pieces[3] + pieces[4] + pieces[5]], axis=1
    )
    top = jnp.max(logs, axis=0, keepdims=True)
    log_total = top + jnp.log(jnp.sum(jnp.exp(logs - top), axis=0, keepdims=True))

    scale = grad[...] * jnp.exp(stat[0:1, :] - log_total)
    label_grad = grad[...] * (jnp.exp(stat[1:2, :] - log_total) - 1.0)
    place = label[...] - section * voc
    line = lax.broadcasted_iota(I32, (CHUNK, tokens), 0)
    copies = []
    for n, k in enumerate(range(0, weight.shape[0], CHUNK)):
        value = soft[k : k + CHUNK, :].astype(F32) * scale
        value = jnp.where(line + k == place, label_grad, value).astype(BF16)
        staged[k : k + CHUNK, :] = jnp.dot(
            value, whole[...], preferred_element_type=F32
        ).astype(BF16)
        at = pl.ds(k, CHUNK)
        copies.append(pltpu.make_async_copy(staged.at[at], weight.at[at], sems.at[n]))
        copies[-1].start()

    target = (
        pieces[6]
        + pltpu.roll(pieces[6], half - SPACE, 1)
        + pltpu.roll(pieces[6], half - 2 * SPACE, 1)
    )
    target = jnp.broadcast_to(jnp.sum(target, axis=0, keepdims=True), (8, half))
    lane = lax.broadcasted_iota(I32, (8, half), 1)
    mine, other = (
        jnp.broadcast_to(x, (8, half)) for x in (log_total[:, :half], log_total[:, half:])
    )
    first = pltpu.roll(mine, (half - mine_n * j) % half, 1) - pltpu.roll(target, half - mine_n, 1)
    second = pltpu.roll(other, (half - mine_n * j) % half, 1) - pltpu.roll(
        target, half - 2 * mine_n, 1
    )
    low = jnp.where(core == 0, first, second)
    high = pltpu.roll(jnp.where(core == 0, second, first), mine_n, 1)
    loss[...] = jnp.where(lane < mine_n, low, high)[:1, : loss.shape[1]]

    back = (half - mine_n * z) % half
    shares = pltpu.roll(jnp.exp(logs[:, :half] - log_total[:, :half]), back, 1)
    label_part = jnp.exp(target - pltpu.roll(mine, back, 1)) - 1.0
    block = [shares] + [label_part] * ((half - n_z) // 8)
    block = jnp.concatenate(block, axis=0).T[:mine_n]
    sublane = lax.broadcasted_iota(I32, (mine_n, 1), 0)
    own_grad = jnp.zeros((mine_n, 1), F32)
    for r in range(mine_n):
        own_grad = jnp.where(sublane == r, loss_grad[section * mine_n + r], own_grad)
    for n in range(tiles):
        part = jnp.zeros((mine_n, LANES), F32)
        row = jnp.zeros((mine_n, LANES), F32)
        for i in range(n_z):
            part += got[i, n * mine_n : (n + 1) * mine_n, :].astype(F32) * block[:, i : i + 1]
            row += got[i, (tiles + n) * mine_n : (tiles + n + 1) * mine_n, :].astype(F32)
        part += row * block[:, n_z : n_z + 1]
        hidden[:, n * LANES : (n + 1) * LANES] = (own_grad * part).astype(BF16)
    for copy in copies:
        copy.wait()


def local(hidden, head_weight, labels, loss_grad):
    voc, feat = head_weight.shape
    mine_n = hidden.shape[0]
    n_dp = lax.axis_size("dp")
    n_sec = lax.axis_size("section")
    n_z = n_sec // 2
    half = n_z * mine_n
    tokens = 2 * half
    share = tokens // n_dp
    section = lax.axis_index("section")
    z, core = section // 2, section % 2
    j = lax.axis_index("dp")
    scalars = jnp.stack([section, z, core, j, jnp.int32(voc), jnp.int32(mine_n)]).astype(I32)
    along_z = [[2 * k + c for k in range(n_z)] for c in range(2)]
    swap = [(i, i ^ 1) for i in range(n_sec)]
    flops = 2 * tokens * voc * feat

    def exchange_z(x):
        return lax.all_to_all(x, "section", 0, 0, tiled=True, axis_index_groups=along_z)

    def exchange_dp(x):
        return lax.all_to_all(x, "dp", 0, 0, tiled=True)

    def own_core_first(x):
        x = x.reshape(n_z, 2, mine_n)
        first = jnp.where(core == 0, x[:, 0], x[:, 1])
        second = jnp.where(core == 0, x[:, 1], x[:, 0])
        return jnp.concatenate([first.reshape(half), second.reshape(half)])

    mine = exchange_z(jnp.broadcast_to(hidden[None], (n_z, mine_n, feat))).reshape(half, feat)
    tall, rows = call(
        prepare_kernel,
        [],
        [head_weight, (own_core_first(labels) - section * voc)[:, None]],
        [((feat, voc), BF16), ((tokens, feat), BF16)],
        flops=flops,
    )
    label_rows = rows[:half] + lax.ppermute(rows[half:], "section", swap)
    ready = lax.optimization_barrier((mine, tall, label_rows, scalars))
    mine, tall, label_rows, scalars = ready
    other = lax.ppermute(mine, "section", swap)

    width = voc + LANES
    (coded,) = call(
        mine_kernel,
        [],
        [mine, tall],
        [((half, width), I16)],
        scratch=[((half, voc), F32)],
        flops=flops // 2,
    )
    coded, whole = call(
        other_kernel,
        [],
        [coded, mine, other, tall],
        [((tokens, width), I16), ((tokens, feat), BF16)],
        scratch=[((half, voc), F32)],
        flops=flops // 2,
    )
    coded = exchange_dp(coded.reshape(n_dp, share, width))
    (message,) = call(
        softmax_kernel,
        [scalars, labels],
        [coded],
        [((n_dp, share, width), BF16)],
        scratch=[((share, voc), F32)],
    )
    got = exchange_dp(message).reshape(tokens, width)

    send, stat = call(
        send_kernel,
        [],
        [got, head_weight],
        [((half + 16, feat), BF16), ((8, tokens), F32)],
        flops=flops // 2,
    )
    theirs = lax.ppermute(send, "section", swap)
    (part,) = call(keep_kernel, [], [got, head_weight], [((half, feat), F32)], flops=flops // 2)
    (message,) = call(
        pair_kernel,
        [scalars],
        [part, stat, theirs, label_rows],
        [((n_z, (2 * feat // LANES + 1) * mine_n, LANES), BF16)],
    )
    last = exchange_z(message)
    soft = got[:, :voc].T
    late = lax.optimization_barrier((labels, loss_grad, message))
    label, grad = own_core_first(late[0])[None], own_core_first(late[1])[None]
    loss, grad_hidden, grad_weight = call(
        tail_kernel,
        [scalars, loss_grad],
        [last, soft, stat, whole, label, grad],
        [((1, share), F32), ((mine_n, feat), BF16), ((voc, feat), BF16)],
        scratch=[((voc, feat), BF16)],
        copies=voc // CHUNK,
        copies_out=True,
        flops=flops,
    )
    return (loss.reshape(share), grad_hidden, grad_weight)


def solution(mesh):
    return jax.shard_map(
        local,
        mesh=mesh,
        in_specs=(P("section", "dp"), P("section", "dp"), P(), P()),
        out_specs=(P("dp"), P("section", "dp"), P("section", "dp")),
        check_vma=False,
    )
```
